256 devices in a mesh: side: 2 (over core), shard: 128 (over z, y, x).
Axes of the slice: x: 4, y: 4, z: 8, core: 2. Of those that a mesh axis runs over, the one named last changes fastest.
Arguments:
- node_table: bfloat16 [2, 65536, 768], P('side', 'shard'), may hold values from -6 to 6
- owner: int32 [2, 32768, 1], P('side', 'shard'), may hold values from 0 to 127; in each aligned block of 256 rows (0 to 255, 256 to 511, ..., all dimensions but the last counted through in order) at most 4 rows name the same one
- local_row: int32 [2, 32768], P('side', 'shard'), may hold values from 0 to 511
- w_in: bfloat16 [2, 768, 1024], P('side'), may hold values from -0.21875 to 0.21875
- w_mid: bfloat16 [2, 1024, 1024], P('side'), may hold values from -0.1875 to 0.1875
- w_out: bfloat16 [2, 1024, 128], P('side'), may hold values from -0.1875 to 0.1875
Outputs:
- grad_in: float32 [2, 768, 1024], P('side')
- grad_mid: float32 [2, 1024, 1024], P('side')
- grad_out: float32 [2, 1024, 128], P('side')
The draws below stay inside these ranges and needn't reach their ends.
Inputs may be any that keep to these rules, and one draw needn't show every extreme that they name: In each tower, among the 256 pairs of one device at most 4 name the same owner, and that bound is reached.
All inputs are finite; a program needn't handle non-finite values.
Results may differ from the reference program's by a relative error of at most 0.0095.
Values may be sent and summed in bfloat16 or wider, within the bound.
No kernel may reach another device: no remote copies, remote signals or barrier semaphores. Data moves between devices by JAX's collectives and lax.ppermute only.
A program may use at most 128 MiB of HBM per device.

```python
import math
import jax
import jax.numpy as jnp
import numpy as np
from jax import lax

FEAT = 768
HID = 1024
EMB = 128
ROWS_DEV = 512
TOK_DEV = 256
CAP = 4
TOKENS = 32768
TABLE = 65536
N_SHARD = 128


def plant(drawn, stream_key, least, high):
    extent = drawn.shape
    spot = [jax.random.randint(jax.random.fold_in(stream_key, axis), (), 0, extent[axis]) for axis in range(len(extent))]
    drawn = drawn.at[tuple(spot)].set(least)
    longest = extent.index(max(extent))
    spot[longest] = (spot[longest] + 1) % extent[longest]
    return drawn.at[tuple(spot)].set(high)


def shard_levels(key, dims, shards, low, largest):
    def one(axis_at, parts):
        steps = jax.random.uniform(jax.random.fold_in(jax.random.fold_in(key, 6), axis_at), (parts,), jnp.float32, low / len(shards), largest / len(shards))
        return jnp.repeat(jnp.exp(steps), dims[axis_at] // parts).reshape((-1,) + (1,) * (len(dims) - axis_at - 1))

    factor_of = one(*shards[0])
    for cut in shards[1:]:
        factor_of = factor_of * one(*cut)
    return factor_of


def routed_block(stream_key, own, number, rows, number_of, top, reach, skew):
    sequence = jax.random.permutation(stream_key, number_of)
    packed, common = shares(number_of, rows * top, reach, skew, True), shares(number_of, rows * top, reach, skew, False)
    places = jnp.arange(number_of)

    def named(tallies, rotation):
        used = int((tallies > 0).sum())
        fixed = max(1, used // 4)
        shifted = fixed + (places - fixed + rotation * (used - fixed)) % max(1, number_of - fixed)
        return jnp.zeros((number_of,), jnp.int32).at[sequence[jnp.where(places < fixed, places, shifted)]].set(jnp.asarray(tallies, jnp.int32))

    tallies = jnp.where(number % 4 == 0, named(packed, number // 4), named(common, number - number // 4 - 1))
    mixed = jax.random.permutation(jax.random.fold_in(own, 3), number_of)
    donor, receiver = mixed[0:number_of // 2 * 2:2], mixed[1:number_of // 2 * 2:2]
    slack = jnp.minimum(tallies[donor] - 1, reach - tallies[receiver]) // 2
    slack = jnp.where((donor == sequence[0]) | (receiver == sequence[0]) | (tallies[receiver] == 0), 0, jnp.maximum(slack, 0))
    shifted = jax.random.randint(jax.random.fold_in(own, 4), (number_of // 2,), 0, 1 << 20) % (slack + 1)
    tallies = tallies.at[donor].add(-shifted).at[receiver].add(shifted)
    members = jnp.searchsorted(jnp.cumsum(tallies), jnp.arange(rows * top), side="right").astype(jnp.int32)
    listing = members.reshape(top, rows).T
    listing = listing[jax.random.permutation(jax.random.fold_in(own, 1), rows)]
    rotation = jax.random.randint(jax.random.fold_in(own, 2), (rows, 1), 0, top)
    return jnp.take_along_axis(listing, (jnp.arange(top)[None, :] + rotation) % top, axis=1)


def shares(number_of, total, reach, lean, full):
    loads = [(1 << 20) // math.isqrt(standing ** lean) + 1 for standing in range(1, number_of + 1)]
    largest = reach if full else min(reach, max(-(-total // number_of), total * loads[0] // sum(loads)))
    least = 1 if total - largest >= number_of - 1 else 0
    holding, spare = [largest] + [least] * (number_of - 1), total - largest - least * (number_of - 1)
    while spare > 0:
        free = [i for i in range(1, number_of) if holding[i] < largest] or [i for i in range(1, number_of) if holding[i] < reach]
        pool, left = sum([loads[i] for i in free]), spare
        for i in free:
            more = min(reach - holding[i], max(1, left * loads[i] // pool), spare)
            holding[i] = holding[i] + more
            spare = spare - more
    return np.array(holding)


def normal_values(stream_key, dims, scale, most, split=(), kind=jnp.bfloat16):
    gain = shard_levels(stream_key, dims, split, -0.22, 0.18) if split else 1.0
    array = jax.random.normal(stream_key, dims, jnp.float32) * scale * gain
    return jnp.minimum(jnp.maximum(array, -most), most).astype(kind)


def setup_inputs(seed: int = 0) -> dict:
    seeds = jax.random.split(jax.random.key(seed), 7)
    node_table = normal_values(seeds[0], (2, TABLE, FEAT), 1.0, 6.0, ((0, 2), (1, 128)))
    owner_keys = jax.random.split(jax.random.fold_in(seeds[1], 1), 2 * TOKENS // TOK_DEV)
    owner_turns = jax.random.permutation(jax.random.fold_in(seeds[1], 3), 2 * TOKENS // TOK_DEV)
    owner = jax.vmap(lambda own, number: routed_block(jax.random.fold_in(seeds[1], 2), own, number, TOK_DEV, N_SHARD, 1, CAP, 2))(owner_keys, owner_turns).reshape((2, TOKENS, 1))
    local_row = plant(jax.random.randint(seeds[2], (2, TOKENS), 0, ROWS_DEV), jax.random.fold_in(seeds[2], 1), 0, ROWS_DEV - 1).astype(jnp.int32)
    w_in = normal_values(seeds[3], (2, FEAT, HID), FEAT ** -0.5, 0.21875, ((0, 2),))
    w_mid = normal_values(seeds[4], (2, HID, HID), HID ** -0.5, 0.1875, ((0, 2),))
    w_out = normal_values(seeds[5], (2, HID, EMB), HID ** -0.5, 0.1875, ((0, 2),))
    return dict(node_table=node_table, owner=owner, local_row=local_row, w_in=w_in, w_mid=w_mid, w_out=w_out)


def silu_slope(argument):
    logistic = jax.nn.sigmoid(argument)
    return logistic * (1.0 + argument * (1.0 - logistic))

def tower(features, weight_in, weight_mid, weight_out):
    pre_one = jnp.dot(features, weight_in, preferred_element_type=jnp.float32)
    hidden_one = jax.nn.silu(pre_one).astype(jnp.bfloat16)
    pre_two = jnp.dot(hidden_one, weight_mid, preferred_element_type=jnp.float32)
    hidden_two = jax.nn.silu(pre_two).astype(jnp.bfloat16)
    pre_three = jnp.dot(hidden_two, weight_out, preferred_element_type=jnp.float32)
    inverse_norm = lax.rsqrt(lax.optimization_barrier(jnp.sum(pre_three * pre_three, axis=-1, keepdims=True)) + 1e-06)
    unit_emb = pre_three * inverse_norm
    saved = (pre_one, hidden_one, pre_two, hidden_two, inverse_norm, unit_emb)
    return (saved, unit_emb.astype(jnp.bfloat16))

def tower_grads(features, weight_mid, weight_out, saved, grad_embed):
    pre_one, hidden_one, pre_two, hidden_two, inverse_norm, unit_emb = saved
    along_unit = lax.optimization_barrier(jnp.sum(grad_embed * unit_emb, axis=-1, keepdims=True))
    back_three = ((grad_embed - unit_emb * along_unit) * inverse_norm).astype(jnp.bfloat16)
    back_two = (jnp.dot(back_three, weight_out.T, preferred_element_type=jnp.float32) * silu_slope(pre_two)).astype(jnp.bfloat16)
    back_one = (jnp.dot(back_two, weight_mid.T, preferred_element_type=jnp.float32) * silu_slope(pre_one)).astype(jnp.bfloat16)
    sum_out = jnp.dot(hidden_two.T, back_three, preferred_element_type=jnp.float32)
    sum_mid = jnp.dot(hidden_one.T, back_two, preferred_element_type=jnp.float32)
    sum_in = jnp.dot(features.T, back_one, preferred_element_type=jnp.float32)
    return (sum_in, sum_mid, sum_out)

def contrast(user_emb, item_emb):
    loss_scale = 0.5 / math.sqrt(TOKENS)
    user_blocks = user_emb.reshape(N_SHARD, TOK_DEV, EMB)
    columns = jnp.arange(TOKENS, dtype=jnp.int32)

    def norm_pass(col_total, block):
        expo = jnp.exp(40.0 * jnp.dot(block, item_emb.T, preferred_element_type=jnp.float32))
        return (col_total + lax.optimization_barrier(jnp.sum(expo, axis=0)), jnp.log(lax.optimization_barrier(jnp.sum(expo, axis=1))))
    col_total, row_norms = lax.scan(norm_pass, jnp.zeros((TOKENS,), jnp.float32), user_blocks)
    column_norm = jnp.log(col_total)

    def grad_pass(item_grad, inputs):
        block, row_norm, index = inputs
        scores = 40.0 * jnp.dot(block, item_emb.T, preferred_element_type=jnp.float32)
        own_rows = index * TOK_DEV + jnp.arange(TOK_DEV, dtype=jnp.int32)
        diagonal_mask = (columns[None, :] == own_rows[:, None]).astype(jnp.float32)
        row_grad = ((jnp.exp(scores - row_norm[:, None]) - diagonal_mask) * loss_scale).astype(jnp.bfloat16)
        col_grad = ((jnp.exp(scores - column_norm[None, :]) - diagonal_mask) * loss_scale).astype(jnp.bfloat16)
        joined = row_grad.astype(jnp.float32) + col_grad.astype(jnp.float32)
        user_grad = 40.0 * jnp.dot(joined, item_emb.astype(jnp.float32), preferred_element_type=jnp.float32)
        item_part = 40.0 * jnp.dot(joined.T, block.astype(jnp.float32), preferred_element_type=jnp.float32)
        return (item_grad + item_part, user_grad)
    item_grad, user_grads = lax.scan(grad_pass, jnp.zeros((TOKENS, EMB), jnp.float32), (user_blocks, row_norms, jnp.arange(N_SHARD, dtype=jnp.int32)))
    return (user_grads.reshape(TOKENS, EMB), item_grad)

def reference(node_table, owner, local_row, w_in, w_mid, w_out):
    inputs = []
    saves = []
    embeds = []
    for tower_id in range(2):
        row_ids = (owner[tower_id, :, 0] * ROWS_DEV + local_row[tower_id]).astype(jnp.int32)
        features = jnp.take(node_table[tower_id], row_ids, axis=0)
        saved, embedded = tower(features, w_in[tower_id], w_mid[tower_id], w_out[tower_id])
        inputs.append(features)
        saves.append(saved)
        embeds.append(embedded)
    user_grad, item_grad = contrast(embeds[0], embeds[1])
    grads = [user_grad, item_grad]
    results = []
    for tower_id in range(2):
        results.append(tower_grads(inputs[tower_id], w_mid[tower_id], w_out[tower_id], saves[tower_id], grads[tower_id]))
    grad_in = jnp.stack([results[0][0], results[1][0]])
    grad_mid = jnp.stack([results[0][1], results[1][1]])
    grad_out = jnp.stack([results[0][2], results[1][2]])
    return (grad_in, grad_mid, grad_out)
```

```python
import math

import jax
import jax.numpy as jnp
from jax import lax
from jax.experimental import pallas as pl
from jax.experimental.pallas import tpu as pltpu
from jax.sharding import Mesh, PartitionSpec as P

NZ, NY, NX = 8, 4, 4
NYX = NY * NX
N_SHARD = NZ * NYX
CAP = 4
ROWS_DEV = 512
TOK = 256
HALF = TOK // 2
FEAT, HID, EMB = 768, 1024, 128
TOKENS = N_SHARD * TOK
UROWS = NZ * HALF
ICOLS = NYX * HALF
EXP2_SCALE = 40.0 / math.log(2.0)
GRAD_SCALE = 40.0 * 0.5 / math.sqrt(TOKENS)
WROWS = FEAT + HID + EMB
PIECE = WROWS // NYX
BF16 = jnp.bfloat16
F32 = jnp.float32
VMEM = pl.BlockSpec(memory_space=pltpu.VMEM)
SMEM = pl.BlockSpec(memory_space=pltpu.SMEM)


def call(kernel, outs, in_specs, scratch=(), mib=48):
    return pl.pallas_call(
        kernel,
        out_shape=[jax.ShapeDtypeStruct(s, d) for s, d in outs],
        in_specs=in_specs,
        out_specs=[VMEM] * len(outs),
        scratch_shapes=list(scratch),
        compiler_params=pltpu.CompilerParams(vmem_limit_bytes=mib * 2**20),
    )


def dot(a, b, dims):
    return lax.dot_general(a, b, (dims, ((), ())), preferred_element_type=F32)


NN = ((1,), (0,))
NT = ((1,), (1,))
TN = ((0,), (0,))


def iota(shape, dim):
    return lax.broadcasted_iota(jnp.int32, shape, dim)


def request_kernel(owner_ref, wanted_ref, request_ref, position_ref):
    own_col = jnp.broadcast_to(owner_ref[...].astype(F32), (TOK, TOK))
    own_row = own_col.T
    earlier = iota((TOK, TOK), 0) < iota((TOK, TOK), 1)
    same = jnp.where((own_col == own_row) & earlier, 1.0, 0.0)
    rank = jnp.sum(same, axis=0, keepdims=True)
    owners = own_row[0:1, :]
    position_ref[...] = (owners * CAP + rank).astype(jnp.int32)
    wanted = wanted_ref[...].astype(F32) + 1.0
    owner_hit = iota((N_SHARD, TOK), 0).astype(F32) == owners
    lanes = iota((N_SHARD, 128), 1)
    request = jnp.zeros((N_SHARD, 128), F32)
    for k in range(CAP):
        hit = jnp.where(owner_hit & (rank == float(k)), wanted, 0.0)
        slot = jnp.sum(hit, axis=1, keepdims=True)
        request = jnp.where(lanes == k, slot, request)
    request_ref[...] = request.astype(jnp.int32) - 1


def pick_kernel(incoming_ref, table_ref, picked_ref):
    slots = N_SHARD * CAP
    spread = jnp.where(iota((slots, N_SHARD), 0) // CAP == iota((slots, N_SHARD), 1), 1.0, 0.0)
    listed = lax.dot_general(
        spread,
        incoming_ref[...].astype(F32),
        (NN, ((), ())),
        precision=lax.Precision.HIGHEST,
        preferred_element_type=F32,
    )
    mine = iota((slots, 128), 0) % CAP == iota((slots, 128), 1)
    row = jnp.sum(jnp.where(mine, listed, 0.0), axis=1, keepdims=True)
    hit = jnp.where(row == iota((slots, ROWS_DEV), 1).astype(F32), 1.0, 0.0).astype(BF16)
    picked_ref[...] = dot(hit, table_ref[...], NN).astype(BF16)


def silu(v):
    return v * (1.0 / (1.0 + jnp.exp(-v)))


def slope(v):
    q = 1.0 / (1.0 + jnp.exp(-v))
    return q * (1.0 + v * (1.0 - q))


def forward_kernel(
    position_ref, arrived_ref, w_in_ref, w_mid_ref, w_out_ref,
    x_ref, z1_ref, z2_ref, u_ref, r_ref, e_ref,
):
    slots = N_SHARD * CAP
    hit = jnp.where(iota((slots, TOK), 0) == position_ref[...], 1.0, 0.0).astype(BF16)
    x = dot(hit, arrived_ref[...], TN).astype(BF16)
    x_ref[...] = x
    z1 = dot(x, w_in_ref[...], NN)
    z1_ref[...] = z1
    z2 = dot(silu(z1).astype(BF16), w_mid_ref[...], NN)
    z2_ref[...] = z2
    z3 = dot(silu(z2).astype(BF16), w_out_ref[...], NN)
    r = lax.rsqrt(jnp.sum(z3 * z3, axis=1, keepdims=True) + 1e-6)
    u = z3 * r
    u_ref[...] = u
    r_ref[...] = jnp.broadcast_to(r, (TOK, EMB))
    e_ref[...] = u.astype(BF16)


CHUNK = 256


def sums_kernel(own_ref, other_ref, items_ref, row_ref, col_ref):
    items = items_ref[...]
    cols = jnp.zeros((8, ICOLS), F32)
    for part, users_ref in ((0, own_ref), (1, other_ref)):
        for c in range(UROWS // CHUNK):
            scores = dot(users_ref[c * CHUNK:(c + 1) * CHUNK, :], items, NT)
            expo = jnp.exp2(scores * EXP2_SCALE)
            cols = cols + jnp.sum(expo.reshape(CHUNK // 8, 8, ICOLS), axis=0)
            folded = expo[:, 0:128]
            for k in range(1, ICOLS // 128):
                folded = folded + expo[:, k * 128:(k + 1) * 128]
            at = part * UROWS + c * CHUNK
            row_ref[:, at:at + CHUNK] = jnp.sum(folded.T, axis=0, keepdims=True)
    col_ref[...] = jnp.sum(cols, axis=0, keepdims=True)


def grad_kernel(
    place_ref, own_ref, other_ref, items_ref, row_ref, col_ref,
    gown_ref, gother_ref, gitems_ref, grad_ref, turned_ref,
):
    items = items_ref[...]
    col_inv = 1.0 / col_ref[...]
    row_inv = 1.0 / row_ref[...]
    z, yx = place_ref[0], place_ref[1]
    for part, users_ref, out_ref in ((0, own_ref, gown_ref), (1, other_ref, gother_ref)):
        for c in range(UROWS // CHUNK):
            users = users_ref[c * CHUNK:(c + 1) * CHUNK, :]
            scores = dot(users, items, NT)
            at = part * UROWS + c * CHUNK
            inv = jnp.broadcast_to(row_inv[:, at:at + CHUNK], (128, CHUNK)).T[:, 0:1]
            grad_ref[...] = jnp.exp2(scores * EXP2_SCALE) * (inv + col_inv)
            if part == 0:
                @pl.when(z // 2 == c)
                def _():
                    rows = pl.ds(pl.multiple_of((z % 2) * HALF, HALF), HALF)
                    columns = pl.ds(pl.multiple_of(yx * HALF, HALF), HALF)
                    eye = iota((HALF, HALF), 0) == iota((HALF, HALF), 1)
                    grad_ref[rows, columns] = grad_ref[rows, columns] - jnp.where(eye, 2.0, 0.0)
            grad = grad_ref[...].astype(BF16)
            pull = dot(grad, items, NN) * GRAD_SCALE
            out_ref[c * CHUNK:(c + 1) * CHUNK, :] = pull.astype(BF16)
            term = dot(users, grad, TN)
            if part == 0 and c == 0:
                turned_ref[...] = term
            else:
                turned_ref[...] += term
    gitems_ref[...] = (turned_ref[...] * GRAD_SCALE).T.astype(BF16)


def backward_kernel(
    place_ref, mine_ref, sent_ref, x_ref, z1_ref, z2_ref, u_ref, r_ref, w_mid_ref, w_out_ref,
    out_ref, sums_ref,
):
    first = place_ref[2] == 0
    mine, sent = mine_ref[...], sent_ref[...]
    g = jnp.concatenate([jnp.where(first, mine, sent), jnp.where(first, sent, mine)], axis=0)
    u = u_ref[...]
    along = jnp.sum(g * u, axis=1, keepdims=True)
    dz3 = ((g - u * along) * r_ref[...]).astype(BF16)
    z2 = z2_ref[...]
    h2 = silu(z2).astype(BF16)
    sums_ref[FEAT + HID:, :] = dot(dz3, h2, TN)
    dz2 = (dot(dz3, w_out_ref[...], NT) * slope(z2)).astype(BF16)
    z1 = z1_ref[...]
    h1 = silu(z1).astype(BF16)
    sums_ref[FEAT:FEAT + HID, :] = dot(h1, dz2, TN)
    dz1 = (dot(dz2, w_mid_ref[...], NT) * slope(z1)).astype(BF16)
    sums_ref[0:FEAT, :] = dot(x_ref[...], dz1, TN)
    for q in range(NYX):
        rows = sums_ref[q * PIECE:(q + 1) * PIECE, :]
        pieces = [rows[:, k * 128:(k + 1) * 128] for k in range(NZ)]
        out_ref[q] = jnp.concatenate(pieces, axis=0).astype(BF16)


def finish_kernel(parts_ref, grad_in_ref, grad_mid_ref, grad_out_ref, turned_ref):
    places = ((0, FEAT, grad_in_ref), (FEAT, FEAT + HID, grad_mid_ref), (FEAT + HID, WROWS, turned_ref))
    for q in range(NYX):
        rows = parts_ref[q].astype(F32)
        for start, stop, ref in places:
            low, high = max(start, q * PIECE), min(stop, (q + 1) * PIECE)
            if low >= high:
                continue
            for k in range(NZ):
                piece = rows[k * PIECE + low - q * PIECE:k * PIECE + high - q * PIECE, :]
                ref[low - start:high - start, k * 128:(k + 1) * 128] = piece
    grad_out_ref[...] = turned_ref[...].T


YX = ("y", "x")
ALL = ("z", "y", "x")


def exchange(value, axes):
    return lax.all_to_all(value, axes, split_axis=0, concat_axis=0, tiled=True)


def spread(value, axes, n):
    return exchange(jnp.broadcast_to(value[None], (n,) + value.shape), axes)


def swap(value):
    return lax.ppermute(value, "side", [(0, 1), (1, 0)])


def total(parts):
    return jnp.sum(parts.astype(F32), axis=0)


def on_device(node_table, owner, local_row, w_in, w_mid, w_out):
    side = lax.axis_index("side")
    place = jnp.stack([lax.axis_index("z"), lax.axis_index("y") * NX + lax.axis_index("x"), side])
    place = place.astype(jnp.int32)
    table, weight_in, weight_mid, weight_out = node_table[0], w_in[0], w_mid[0], w_out[0]

    request, position = call(
        request_kernel,
        [((N_SHARD, 128), jnp.int32), ((1, TOK), jnp.int32)],
        [VMEM, VMEM],
    )(owner[0], local_row)
    incoming = exchange(request.reshape(N_SHARD, 1, 128), ALL).reshape(N_SHARD, 128)
    (picked,) = call(
        pick_kernel, [((N_SHARD * CAP, FEAT), BF16)], [VMEM, VMEM]
    )(incoming, table)
    arrived = exchange(picked.reshape(N_SHARD, CAP, FEAT), ALL).reshape(N_SHARD * CAP, FEAT)
    x, z1, z2, u, r, e = call(
        forward_kernel,
        [
            ((TOK, FEAT), BF16), ((TOK, HID), F32), ((TOK, HID), F32),
            ((TOK, EMB), F32), ((TOK, EMB), F32), ((TOK, EMB), BF16),
        ],
        [VMEM] * 5,
    )(position, arrived, weight_in, weight_mid, weight_out)

    partner = swap(e)
    mine, theirs = jnp.where(side == 0, e, partner), jnp.where(side == 0, partner, e)
    user_half = lax.dynamic_slice_in_dim(mine, side * HALF, HALF, 0)
    item_half = lax.dynamic_slice_in_dim(theirs, side * HALF, HALF, 0)
    own_users = spread(user_half, "z", NZ).reshape(UROWS, EMB)
    other_users = swap(own_users)
    items = spread(item_half, YX, NYX).reshape(ICOLS, EMB)

    row, col = call(
        sums_kernel, [((1, 2 * UROWS), F32), ((1, ICOLS), F32)], [VMEM] * 3
    )(own_users, other_users, items)
    row = row.reshape(2, 8, 128)
    row = row + swap(row)[::-1]
    row = total(spread(row, "z", NZ)).reshape(1, 2 * UROWS)
    col = total(spread(col.reshape(ICOLS // 128, 128), YX, NYX)).reshape(1, ICOLS)

    grad_own, grad_other, grad_items = call(
        grad_kernel,
        [((UROWS, EMB), BF16), ((UROWS, EMB), BF16), ((ICOLS, EMB), BF16)],
        [SMEM] + [VMEM] * 5,
        [pltpu.VMEM((CHUNK, ICOLS), F32), pltpu.VMEM((EMB, ICOLS), F32)],
    )(place, own_users, other_users, items, row, col)
    grad_users = (grad_own.astype(F32) + swap(grad_other).astype(F32)).astype(BF16)
    grad_users = total(exchange(grad_users.reshape(NZ, HALF, EMB), "z"))
    grad_items = total(exchange(grad_items.reshape(NYX, HALF, EMB), YX))
    kept = jnp.where(side == 0, grad_users, grad_items)
    sent = swap(jnp.where(side == 0, grad_items, grad_users))

    (sums,) = call(
        backward_kernel,
        [((NYX, NZ * PIECE, 128), BF16)],
        [SMEM] + [VMEM] * 9,
        [pltpu.VMEM((WROWS, HID), F32)],
    )(place, kept, sent, x, z1, z2, u, r, weight_mid, weight_out)
    sums = total(exchange(sums, YX)).astype(BF16)
    sums = total(exchange(sums.reshape(NZ, PIECE, 128), "z")).astype(BF16)
    sums = spread(sums, "z", NZ).reshape(NZ * PIECE, 128)
    sums = spread(sums, YX, NYX)
    grads = call(
        finish_kernel,
        [((FEAT, HID), F32), ((HID, HID), F32), ((HID, EMB), F32)],
        [VMEM],
        [pltpu.VMEM((EMB, HID), F32)],
    )(sums)
    return tuple(g[None] for g in grads)


def solution(mesh):
    cube = Mesh(mesh.devices.reshape(2, NZ, NY, NX), ("side", "z", "y", "x"))
    rows = P("side", ALL, None)
    whole = P("side", None, None)
    return jax.shard_map(
        on_device,
        mesh=cube,
        in_specs=(rows, rows, P("side", ALL), whole, whole, whole),
        out_specs=(whole, whole, whole),
        check_vma=False,
    )
```

```python
import math

import jax
import jax.numpy as jnp
from jax import lax
from jax.experimental import pallas as pl
from jax.experimental.pallas import tpu as pltpu
from jax.sharding import Mesh, PartitionSpec as P

NZ, NY, NX = 8, 4, 4
NYX = NY * NX
N_SHARD = NZ * NYX
CAP = 4
ROWS_DEV = 512
TOK = 256
HALF = TOK // 2
FEAT, HID, EMB = 768, 1024, 128
TOKENS = N_SHARD * TOK
UROWS = NZ * HALF
ICOLS = NYX * HALF
EXP2_SCALE = 40.0 / math.log(2.0)
GRAD_SCALE = 40.0 * 0.5 / math.sqrt(TOKENS)
WROWS = FEAT + HID + EMB
PARTS = 3
PROWS = WROWS // PARTS
LANES = HID // 128
PIECE = PROWS * LANES // N_SHARD
BF16 = jnp.bfloat16
F32 = jnp.float32
VMEM = pl.BlockSpec(memory_space=pltpu.VMEM)
SMEM = pl.BlockSpec(memory_space=pltpu.SMEM)


def call(kernel, outs, in_specs, scratch=(), mib=48, out_space=pltpu.VMEM):
    return pl.pallas_call(
        kernel,
        out_shape=[jax.ShapeDtypeStruct(s, d) for s, d in outs],
        in_specs=in_specs,
        out_specs=[pl.BlockSpec(memory_space=out_space)] * len(outs),
        scratch_shapes=list(scratch),
        compiler_params=pltpu.CompilerParams(vmem_limit_bytes=mib * 2**20),
    )


def dot(a, b, dims):
    return lax.dot_general(a, b, (dims, ((), ())), preferred_element_type=F32)


NN = ((1,), (0,))
NT = ((1,), (1,))
TN = ((0,), (0,))


def iota(shape, dim):
    return lax.broadcasted_iota(jnp.int32, shape, dim)


def request_kernel(owner_ref, wanted_ref, request_ref, position_ref):
    own_col = jnp.broadcast_to(owner_ref[...].astype(F32), (TOK, TOK))
    own_row = own_col.T
    earlier = iota((TOK, TOK), 0) < iota((TOK, TOK), 1)
    same = jnp.where((own_col == own_row) & earlier, 1.0, 0.0)
    rank = jnp.sum(same, axis=0, keepdims=True)
    owners = own_row[0:1, :]
    position_ref[...] = (owners * CAP + rank).astype(jnp.int32)
    wanted = wanted_ref[...].astype(F32) + 1.0
    owner_hit = iota((N_SHARD, TOK), 0).astype(F32) == owners
    lanes = iota((N_SHARD, 128), 1)
    request = jnp.zeros((N_SHARD, 128), F32)
    for k in range(CAP):
        hit = jnp.where(owner_hit & (rank == float(k)), wanted, 0.0)
        slot = jnp.sum(hit, axis=1, keepdims=True)
        request = jnp.where(lanes == k, slot, request)
    request_ref[...] = request.astype(jnp.int32) - 1


def pick_kernel(incoming_ref, table_ref, picked_ref):
    slots = N_SHARD * CAP
    spread = jnp.where(iota((slots, N_SHARD), 0) // CAP == iota((slots, N_SHARD), 1), 1.0, 0.0)
    listed = lax.dot_general(
        spread,
        incoming_ref[...].astype(F32),
        (NN, ((), ())),
        precision=lax.Precision.HIGHEST,
        preferred_element_type=F32,
    )
    mine = iota((slots, 128), 0) % CAP == iota((slots, 128), 1)
    row = jnp.sum(jnp.where(mine, listed, 0.0), axis=1, keepdims=True)
    hit = jnp.where(row == iota((slots, ROWS_DEV), 1).astype(F32), 1.0, 0.0).astype(BF16)
    picked_ref[...] = dot(hit, table_ref[...], NN).astype(BF16)


def silu(v):
    return v * (1.0 / (1.0 + jnp.exp(-v)))


def slope(v):
    q = 1.0 / (1.0 + jnp.exp(-v))
    return q * (1.0 + v * (1.0 - q))


def forward_kernel(
    position_ref, arrived_ref, w_in_ref, w_mid_ref, w_out_ref,
    x_ref, z1_ref, z2_ref, u_ref, r_ref, e_ref,
):
    slots = N_SHARD * CAP
    hit = jnp.where(iota((slots, TOK), 0) == position_ref[...], 1.0, 0.0).astype(BF16)
    x = dot(hit, arrived_ref[...], TN).astype(BF16)
    x_ref[...] = x
    z1 = dot(x, w_in_ref[...], NN)
    z1_ref[...] = z1
    z2 = dot(silu(z1).astype(BF16), w_mid_ref[...], NN)
    z2_ref[...] = z2
    z3 = dot(silu(z2).astype(BF16), w_out_ref[...], NN)
    r = lax.rsqrt(jnp.sum(z3 * z3, axis=1, keepdims=True) + 1e-6)
    u = z3 * r
    u_ref[...] = u
    r_ref[...] = jnp.broadcast_to(r, (TOK, EMB))
    e_ref[...] = u.astype(BF16)


CHUNK = 256


def sums_kernel(own_ref, other_ref, items_ref, row_ref, col_ref):
    items = items_ref[...]
    cols = jnp.zeros((8, ICOLS), F32)
    for part, users_ref in ((0, own_ref), (1, other_ref)):
        for c in range(UROWS // CHUNK):
            scores = dot(users_ref[c * CHUNK:(c + 1) * CHUNK, :], items, NT)
            expo = jnp.exp2(scores * EXP2_SCALE)
            cols = cols + jnp.sum(expo.reshape(CHUNK // 8, 8, ICOLS), axis=0)
            folded = expo[:, 0:128]
            for k in range(1, ICOLS // 128):
                folded = folded + expo[:, k * 128:(k + 1) * 128]
            sums = jnp.sum(folded.T, axis=0, keepdims=True)
            for k in range(CHUNK // 128):
                at = (part * UROWS + c * CHUNK) // 128 + k
                row_ref[at] = sums[:, k * 128:(k + 1) * 128]
    col_ref[...] = jnp.sum(cols, axis=0, keepdims=True)


def grad_kernel(
    place_ref, own_ref, other_ref, items_ref, row_ref, col_ref,
    gown_ref, gother_ref, gitems_ref, grad_ref, turned_ref,
):
    items = items_ref[...]
    col_inv = 1.0 / col_ref[...]
    for part, users_ref, out_ref in ((0, own_ref, gown_ref), (1, other_ref, gother_ref)):
        for c in range(UROWS // CHUNK):
            users = users_ref[c * CHUNK:(c + 1) * CHUNK, :]
            scores = dot(users, items, NT)
            at = (part * UROWS + c * CHUNK) // 128
            totals = jnp.concatenate([row_ref[at + k] for k in range(CHUNK // 128)], axis=1)
            inv = jnp.broadcast_to(1.0 / totals, (128, CHUNK)).T[:, 0:1]
            grad_ref[...] = jnp.exp2(scores * EXP2_SCALE) * (inv + col_inv)
            if part == 0 and c == 0:
                columns = pl.ds(pl.multiple_of(place_ref[0] * HALF, HALF), HALF)
                eye = iota((HALF, HALF), 0) == iota((HALF, HALF), 1)
                grad_ref[0:HALF, columns] = grad_ref[0:HALF, columns] - jnp.where(eye, 2.0, 0.0)
            grad = grad_ref[...].astype(BF16)
            pull = dot(grad, items, NN) * GRAD_SCALE
            out_ref[c * CHUNK:(c + 1) * CHUNK, :] = pull.astype(out_ref.dtype)
            term = dot(users, grad, TN)
            if part == 0 and c == 0:
                turned_ref[...] = term
            else:
                turned_ref[...] += term
    gitems_ref[...] = (turned_ref[...] * GRAD_SCALE).T.astype(BF16)


def piece_at(part, slot, code):
    piece = slot ^ code
    row = pl.multiple_of(part * PROWS + lax.shift_right_logical(piece, 3) * PIECE, 8)
    lane = pl.multiple_of(lax.bitwise_and(piece, LANES - 1) * 128, 128)
    return pl.ds(row, PIECE), pl.ds(lane, 128)


SLOTS = N_SHARD // 2


def backward_kernel(
    place_ref, mine_ref, sent_ref, x_ref, z1_ref, z2_ref, u_ref, r_ref, w_mid_ref, w_out_ref,
    *rest,
):
    send_refs, keep_refs, sums_ref = rest[:PARTS], rest[PARTS:2 * PARTS], rest[2 * PARTS]
    first = place_ref[1] == 0
    mine, sent = mine_ref[...], sent_ref[...]
    g = jnp.concatenate([jnp.where(first, mine, sent), jnp.where(first, sent, mine)], axis=0)
    u = u_ref[...]
    along = jnp.sum(g * u, axis=1, keepdims=True)
    dz3 = ((g - u * along) * r_ref[...]).astype(BF16)
    z2 = z2_ref[...]
    h2 = silu(z2).astype(BF16)
    sums_ref[FEAT + HID:, :] = dot(dz3, h2, TN)
    dz2 = (dot(dz3, w_out_ref[...], NT) * slope(z2)).astype(BF16)
    z1 = z1_ref[...]
    h1 = silu(z1).astype(BF16)
    sums_ref[FEAT:FEAT + HID, :] = dot(h1, dz2, TN)
    dz1 = (dot(dz2, w_mid_ref[...], NT) * slope(z1)).astype(BF16)
    sums_ref[0:FEAT, :] = dot(x_ref[...], dz1, TN)
    for part in range(PARTS):
        code = place_ref[2 + part]
        for slot in range(SLOTS):
            keep_refs[part][slot] = sums_ref[piece_at(part, slot, code)]
            send_refs[part][slot] = sums_ref[piece_at(part, SLOTS + slot, code)].astype(BF16)


def finish_kernel(place_ref, *rest):
    halves, outs = rest[:2 * PARTS], rest[2 * PARTS:2 * PARTS + 3]
    sums_ref, turned_ref, sems = rest[2 * PARTS + 3:]
    copies = []

    def send(source, out):
        copies.append(pltpu.make_async_copy(source, out, sems.at[len(copies)]))
        copies[-1].start()

    for part in range(PARTS):
        code = place_ref[2 + part]
        for half in range(2):
            for slot in range(SLOTS):
                piece = halves[2 * part + half][slot].astype(F32)
                sums_ref[piece_at(part, half * SLOTS + slot, code)] = piece
        for k, (start, stop) in enumerate(((0, FEAT), (FEAT, FEAT + HID))):
            low, high = max(start, part * PROWS), min(stop, (part + 1) * PROWS)
            if low < high:
                send(sums_ref.at[low:high, :], outs[k].at[low - start:high - start, :])
    turned_ref[...] = sums_ref[FEAT + HID:, :].T
    send(turned_ref, outs[2])
    for copy in copies:
        copy.wait()


YX = ("y", "x")
ALL = ("z", "y", "x")


def exchange(value, axes):
    return lax.all_to_all(value, axes, split_axis=0, concat_axis=0, tiled=True)


def spread(value, axes, n):
    return exchange(jnp.broadcast_to(value[None], (n,) + value.shape), axes)


def swap(value):
    return lax.ppermute(value, "side", [(0, 1), (1, 0)])


def total(parts):
    return jnp.sum(parts.astype(F32), axis=0)


SIZES = {"x": NX, "y": NY, "z": NZ}


def gray(i):
    return i ^ (i >> 1)


def across(value, axis, bit):
    at = {gray(i): i for i in range(SIZES[axis])}
    return lax.ppermute(value, axis, [(i, at[gray(i) ^ (1 << bit)]) for i in range(SIZES[axis])])


USER_STEPS = (1, 2, 0)
HEADS = (("x", 0), ("y", 0), ("z", 0))
TAIL = (("x", 1), ("y", 1), ("z", 2), ("z", 1))


def steps_of(part):
    return HEADS[part:] + HEADS[:part] + TAIL


def halves(value, axis=0):
    n = value.shape[axis] // 2
    return (
        lax.slice_in_dim(value, 0, n, axis=axis),
        lax.slice_in_dim(value, n, 2 * n, axis=axis).astype(BF16),
    )


def sum_weights(sends, keeps):
    sums = []
    for part in range(PARTS):
        keep, send = keeps[part], sends[part]
        for step in range(len(HEADS)):
            value = keep + across(send, *steps_of(part)[step]).astype(F32)
            if step < len(HEADS) - 1:
                keep, send = halves(value)
        sums.append(value)
    value = jnp.stack(sums)
    for step in TAIL:
        keep, send = halves(value, 1)
        value = keep + across(send, *step).astype(F32)
    return value.astype(BF16)


def spread_weights(value):
    for step in TAIL[::-1]:
        value = jnp.concatenate([value, across(value, *step)], axis=1)
    pairs = []
    for part in range(PARTS):
        mine = value[part]
        heads = steps_of(part)[:len(HEADS)][::-1]
        for step in heads[:-1]:
            mine = jnp.concatenate([mine, across(mine, *step)], axis=0)
        pairs += [mine, across(mine, *heads[-1])]
    return pairs


def on_device(node_table, owner, local_row, w_in, w_mid, w_out):
    side = lax.axis_index("side")
    codes = {axis: gray(lax.axis_index(axis)) for axis in SIZES}
    marks = []
    for part in range(PARTS):
        code = 0
        for axis, bit in steps_of(part):
            code = code * 2 + ((codes[axis] >> bit) & 1)
        marks.append(code)
    yx = lax.axis_index("y") * NX + lax.axis_index("x")
    place = jnp.stack([yx, side] + marks).astype(jnp.int32)
    table, weight_in, weight_mid, weight_out = node_table[0], w_in[0], w_mid[0], w_out[0]

    request, position = call(
        request_kernel,
        [((N_SHARD, 128), jnp.int32), ((1, TOK), jnp.int32)],
        [VMEM, VMEM],
    )(owner[0], local_row)
    incoming = exchange(request.reshape(N_SHARD, 1, 128), ALL).reshape(N_SHARD, 128)
    (picked,) = call(
        pick_kernel, [((N_SHARD * CAP, FEAT), BF16)], [VMEM, VMEM]
    )(incoming, table)
    arrived = exchange(picked.reshape(N_SHARD, CAP, FEAT), ALL).reshape(N_SHARD * CAP, FEAT)
    x, z1, z2, u, r, e = call(
        forward_kernel,
        [
            ((TOK, FEAT), BF16), ((TOK, HID), F32), ((TOK, HID), F32),
            ((TOK, EMB), F32), ((TOK, EMB), F32), ((TOK, EMB), BF16),
        ],
        [VMEM] * 5,
    )(position, arrived, weight_in, weight_mid, weight_out)

    partner = swap(e)
    mine, theirs = jnp.where(side == 0, e, partner), jnp.where(side == 0, partner, e)
    user_half = lax.dynamic_slice_in_dim(mine, side * HALF, HALF, 0)
    item_half = lax.dynamic_slice_in_dim(theirs, side * HALF, HALF, 0)
    items = spread(item_half, YX, NYX).reshape(ICOLS, EMB)
    own_users = user_half[None]
    for bit in USER_STEPS:
        own_users = jnp.concatenate([own_users, across(own_users, "z", bit)])
    own_users = own_users.reshape(UROWS, EMB)
    other_users = swap(own_users)

    row, col = call(
        sums_kernel, [((2 * NZ, 1, 128), F32), ((1, ICOLS), F32)], [VMEM] * 3
    )(own_users, other_users, items)
    col = total(spread(col.reshape(ICOLS // 128, 128), YX, NYX)).reshape(1, ICOLS)
    row = row.reshape(2, 2, 2, 2, 1, 128)
    row = row + jnp.flip(swap(row), 0)
    for k, bit in enumerate(USER_STEPS[::-1]):
        row = row + jnp.flip(across(row, "z", bit), k + 1)
    row = row.reshape(2 * NZ, 1, 128)

    grad_own, grad_other, grad_items = call(
        grad_kernel,
        [((UROWS, EMB), F32), ((UROWS, EMB), BF16), ((ICOLS, EMB), BF16)],
        [SMEM] + [VMEM] * 5,
        [pltpu.VMEM((CHUNK, ICOLS), F32), pltpu.VMEM((EMB, ICOLS), F32)],
    )(place, own_users, other_users, items, row, col)
    grad_items = total(exchange(grad_items.reshape(NYX, HALF, EMB), YX))
    grad_users = grad_own + swap(grad_other).astype(F32)
    for bit in USER_STEPS[::-1]:
        keep, send = halves(grad_users)
        grad_users = keep + across(send, "z", bit).astype(F32)
    kept = jnp.where(side == 0, grad_users, grad_items)
    sent = swap(jnp.where(side == 0, grad_items, grad_users))

    slots = (SLOTS, PIECE, 128)
    sums = call(
        backward_kernel,
        [(slots, BF16)] * PARTS + [(slots, F32)] * PARTS,
        [SMEM] + [VMEM] * 9,
        [pltpu.VMEM((WROWS, HID), F32)],
    )(place, kept, sent, x, z1, z2, u, r, weight_mid, weight_out)
    pairs = spread_weights(sum_weights(sums[:PARTS], sums[PARTS:]))
    grads = call(
        finish_kernel,
        [((FEAT, HID), F32), ((HID, HID), F32), ((HID, EMB), F32)],
        [SMEM] + [VMEM] * (2 * PARTS),
        [pltpu.VMEM((WROWS, HID), F32), pltpu.VMEM((HID, EMB), F32), pltpu.SemaphoreType.DMA((5,))],
        out_space=pl.ANY,
    )(place, *pairs)
    return tuple(g[None] for g in grads)


def solution(mesh):
    cube = Mesh(mesh.devices.reshape(2, NZ, NY, NX), ("side", "z", "y", "x"))
    rows = P("side", ALL, None)
    whole = P("side", None, None)
    return jax.shard_map(
        on_device,
        mesh=cube,
        in_specs=(rows, rows, P("side", ALL), whole, whole, whole),
        out_specs=(whole, whole, whole),
        check_vma=False,
    )
```

```python
import itertools
import math

import jax
import jax.numpy as jnp
from jax import lax
from jax.experimental import pallas as pl
from jax.experimental.pallas import tpu as pltpu
from jax.sharding import Mesh, PartitionSpec as P

NZ, NY, NX = 8, 4, 4
NYX = NY * NX
N_SHARD = NZ * NYX
CAP = 4
ROWS_DEV = 512
TOK = 256
HALF = TOK // 2
FEAT, HID, EMB = 768, 1024, 128
TOKENS = N_SHARD * TOK
UROWS = NZ * HALF
ICOLS = NYX * HALF
EXP2_SCALE = 40.0 / math.log(2.0)
GRAD_SCALE = 40.0 * 0.5 / math.sqrt(TOKENS)
WROWS = FEAT + HID + EMB
PARTS = 3
PROWS = WROWS // PARTS
LANES = HID // 128
PIECE = PROWS * LANES // N_SHARD
BF16 = jnp.bfloat16
F32 = jnp.float32
VMEM = pl.BlockSpec(memory_space=pltpu.VMEM)
SMEM = pl.BlockSpec(memory_space=pltpu.SMEM)


def call(kernel, outs, in_specs, scratch=(), mib=48, out_space=pltpu.VMEM):
    return pl.pallas_call(
        kernel,
        out_shape=[jax.ShapeDtypeStruct(s, d) for s, d in outs],
        in_specs=in_specs,
        out_specs=[pl.BlockSpec(memory_space=out_space)] * len(outs),
        scratch_shapes=list(scratch),
        compiler_params=pltpu.CompilerParams(vmem_limit_bytes=mib * 2**20),
    )


def dot(a, b, dims):
    return lax.dot_general(a, b, (dims, ((), ())), preferred_element_type=F32)


NN = ((1,), (0,))
NT = ((1,), (1,))
TN = ((0,), (0,))


def iota(shape, dim):
    return lax.broadcasted_iota(jnp.int32, shape, dim)


def request_kernel(owner_ref, wanted_ref, request_ref, position_ref):
    own_col = jnp.broadcast_to(owner_ref[...].astype(F32), (TOK, TOK))
    own_row = own_col.T
    earlier = iota((TOK, TOK), 0) < iota((TOK, TOK), 1)
    same = jnp.where((own_col == own_row) & earlier, 1.0, 0.0)
    rank = jnp.sum(same, axis=0, keepdims=True)
    owners = own_row[0:1, :]
    position_ref[...] = (owners * CAP + rank).astype(jnp.int32)
    wanted = wanted_ref[...].astype(F32) + 1.0
    owner_hit = iota((N_SHARD, TOK), 0).astype(F32) == owners
    lanes = iota((N_SHARD, 128), 1)
    request = jnp.zeros((N_SHARD, 128), F32)
    for k in range(CAP):
        hit = jnp.where(owner_hit & (rank == float(k)), wanted, 0.0)
        slot = jnp.sum(hit, axis=1, keepdims=True)
        request = jnp.where(lanes == k, slot, request)
    request_ref[...] = request.astype(jnp.int32) - 1


def pick_kernel(incoming_ref, table_ref, picked_ref):
    slots = N_SHARD * CAP
    spread = jnp.where(iota((slots, N_SHARD), 0) // CAP == iota((slots, N_SHARD), 1), 1.0, 0.0)
    listed = lax.dot_general(
        spread,
        incoming_ref[...].astype(F32),
        (NN, ((), ())),
        precision=lax.Precision.HIGHEST,
        preferred_element_type=F32,
    )
    mine = iota((slots, 128), 0) % CAP == iota((slots, 128), 1)
    row = jnp.sum(jnp.where(mine, listed, 0.0), axis=1, keepdims=True)
    hit = jnp.where(row == iota((slots, ROWS_DEV), 1).astype(F32), 1.0, 0.0).astype(BF16)
    picked_ref[...] = dot(hit, table_ref[...], NN).astype(BF16)


def silu(v):
    return v * (1.0 / (1.0 + jnp.exp(-v)))


def slope(v):
    q = 1.0 / (1.0 + jnp.exp(-v))
    return q * (1.0 + v * (1.0 - q))


def forward_kernel(
    position_ref, arrived_ref, w_in_ref, w_mid_ref, w_out_ref,
    x_ref, z1_ref, z2_ref, u_ref, r_ref, e_ref,
):
    slots = N_SHARD * CAP
    hit = jnp.where(iota((slots, TOK), 0) == position_ref[...], 1.0, 0.0).astype(BF16)
    x = dot(hit, arrived_ref[...], TN).astype(BF16)
    x_ref[...] = x
    z1 = dot(x, w_in_ref[...], NN)
    z1_ref[...] = z1
    z2 = dot(silu(z1).astype(BF16), w_mid_ref[...], NN)
    z2_ref[...] = z2
    z3 = dot(silu(z2).astype(BF16), w_out_ref[...], NN)
    r = lax.rsqrt(jnp.sum(z3 * z3, axis=1, keepdims=True) + 1e-6)
    u = z3 * r
    u_ref[...] = u
    r_ref[...] = jnp.broadcast_to(r, (TOK, EMB))
    e_ref[...] = u.astype(BF16)


CHUNK = 256


def sums_kernel(own_ref, other_ref, items_ref, row_ref, col_ref):
    items = items_ref[...]
    cols = jnp.zeros((8, ICOLS), F32)
    for part, users_ref in ((0, own_ref), (1, other_ref)):
        for c in range(UROWS // CHUNK):
            scores = dot(users_ref[c * CHUNK:(c + 1) * CHUNK, :], items, NT)
            expo = jnp.exp2(scores * EXP2_SCALE)
            cols = cols + jnp.sum(expo.reshape(CHUNK // 8, 8, ICOLS), axis=0)
            folded = expo[:, 0:128]
            for k in range(1, ICOLS // 128):
                folded = folded + expo[:, k * 128:(k + 1) * 128]
            sums = jnp.sum(folded.T, axis=0, keepdims=True)
            for k in range(CHUNK // 128):
                at = (part * UROWS + c * CHUNK) // 128 + k
                row_ref[at] = sums[:, k * 128:(k + 1) * 128]
    col_ref[...] = jnp.sum(cols, axis=0, keepdims=True)


def grad_kernel(
    place_ref, own_ref, other_ref, items_ref, row_ref, col_ref,
    gown_ref, gother_ref, gitems_ref, grad_ref, turned_ref,
):
    items = items_ref[...]
    col_inv = 1.0 / col_ref[...]
    for part, users_ref, out_ref in ((0, own_ref, gown_ref), (1, other_ref, gother_ref)):
        for c in range(UROWS // CHUNK):
            users = users_ref[c * CHUNK:(c + 1) * CHUNK, :]
            scores = dot(users, items, NT)
            at = (part * UROWS + c * CHUNK) // 128
            totals = jnp.concatenate([row_ref[at + k] for k in range(CHUNK // 128)], axis=1)
            inv = jnp.broadcast_to(1.0 / totals, (128, CHUNK)).T[:, 0:1]
            grad_ref[...] = jnp.exp2(scores * EXP2_SCALE) * (inv + col_inv)
            if part == 0 and c == 0:
                columns = pl.ds(pl.multiple_of(place_ref[0] * HALF, HALF), HALF)
                eye = iota((HALF, HALF), 0) == iota((HALF, HALF), 1)
                grad_ref[0:HALF, columns] = grad_ref[0:HALF, columns] - jnp.where(eye, 2.0, 0.0)
            grad = grad_ref[...].astype(BF16)
            pull = dot(grad, items, NN) * GRAD_SCALE
            out_ref[c * CHUNK:(c + 1) * CHUNK, :] = pull.astype(out_ref.dtype)
            term = dot(users, grad, TN)
            if part == 0 and c == 0:
                turned_ref[...] = term
            else:
                turned_ref[...] += term
    gitems_ref[...] = (turned_ref[...] * GRAD_SCALE).T.astype(BF16)


def piece_at(part, slot, code):
    piece = slot ^ code
    row = pl.multiple_of(part * PROWS + lax.shift_right_logical(piece, 3) * PIECE, 8)
    lane = pl.multiple_of(lax.bitwise_and(piece, LANES - 1) * 128, 128)
    return pl.ds(row, PIECE), pl.ds(lane, 128)


SLOTS = N_SHARD // 2


def backward_kernel(
    place_ref, mine_ref, sent_ref, x_ref, z1_ref, z2_ref, u_ref, r_ref, w_mid_ref, w_out_ref,
    *rest,
):
    send_refs, keep_refs, sums_ref = rest[:PARTS], rest[PARTS:2 * PARTS], rest[2 * PARTS]
    first = place_ref[1] == 0
    mine, sent = mine_ref[...], sent_ref[...]
    g = jnp.concatenate([jnp.where(first, mine, sent), jnp.where(first, sent, mine)], axis=0)
    u = u_ref[...]
    along = jnp.sum(g * u, axis=1, keepdims=True)
    dz3 = ((g - u * along) * r_ref[...]).astype(BF16)
    z2 = z2_ref[...]
    h2 = silu(z2).astype(BF16)
    sums_ref[FEAT + HID:, :] = dot(dz3, h2, TN)
    dz2 = (dot(dz3, w_out_ref[...], NT) * slope(z2)).astype(BF16)
    z1 = z1_ref[...]
    h1 = silu(z1).astype(BF16)
    sums_ref[FEAT:FEAT + HID, :] = dot(h1, dz2, TN)
    dz1 = (dot(dz2, w_mid_ref[...], NT) * slope(z1)).astype(BF16)
    sums_ref[0:FEAT, :] = dot(x_ref[...], dz1, TN)
    for part in range(PARTS):
        code = place_ref[2 + part]
        for slot in range(SLOTS):
            keep_refs[part][slot] = sums_ref[piece_at(part, slot, code)]
            send_refs[part][slot] = sums_ref[piece_at(part, SLOTS + slot, code)].astype(BF16)


def finish_kernel(place_ref, *rest):
    halves, outs = rest[:2 * PARTS], rest[2 * PARTS:2 * PARTS + 3]
    sums_ref, turned_ref, sems = rest[2 * PARTS + 3:]
    copies = []

    def send(source, out):
        copies.append(pltpu.make_async_copy(source, out, sems.at[len(copies)]))
        copies[-1].start()

    for part in range(PARTS):
        code = place_ref[2 + part]
        for half in range(2):
            for slot in range(SLOTS):
                piece = halves[2 * part + half][slot].astype(F32)
                sums_ref[piece_at(part, half * SLOTS + slot, code)] = piece
        for k, (start, stop) in enumerate(((0, FEAT), (FEAT, FEAT + HID))):
            low, high = max(start, part * PROWS), min(stop, (part + 1) * PROWS)
            if low < high:
                send(sums_ref.at[low:high, :], outs[k].at[low - start:high - start, :])
    turned_ref[...] = sums_ref[FEAT + HID:, :].T
    send(turned_ref, outs[2])
    for copy in copies:
        copy.wait()


YX = ("y", "x")
ALL = ("z", "y", "x")


def exchange(value, axes):
    return lax.all_to_all(value, axes, split_axis=0, concat_axis=0, tiled=True)


def spread(value, axes, n):
    return exchange(jnp.broadcast_to(value[None], (n,) + value.shape), axes)


def swap(value):
    return lax.ppermute(value, "side", [(0, 1), (1, 0)])


def total(parts):
    return jnp.sum(parts.astype(F32), axis=0)


SIZES = {"x": NX, "y": NY, "z": NZ}


def gray(i):
    return i ^ (i >> 1)


def across(value, axis, bit):
    at = {gray(i): i for i in range(SIZES[axis])}
    return lax.ppermute(value, axis, [(i, at[gray(i) ^ (1 << bit)]) for i in range(SIZES[axis])])


def code_of(i, side, n):
    return gray((i + side) % n)


def trade(value, **flips):
    sizes = [SIZES[axis] for axis in ALL]
    pairs = []
    numbers = {place: k for k, place in enumerate(itertools.product(range(2), *map(range, sizes)))}
    for place, number in numbers.items():
        other = [place[0]]
        for axis, i, n in zip(ALL, place[1:], sizes):
            at = {code_of(k, place[0], n): k for k in range(n)}
            other.append(at[code_of(i, place[0], n) ^ flips.get(axis, 0)])
        pairs.append((number, numbers[tuple(other)]))
    return lax.ppermute(value, ("side",) + ALL, pairs)


USER_STEPS = (1, 2, 0)
PLANE_FOURS = (dict(y=2), dict(x=2), dict(x=2, y=2))
TAIL_FOURS = (dict(z=2), dict(z=4), dict(z=6))
HEADS = (dict(x=1), dict(y=1), dict(z=1))
TAIL = (("x", 1), ("y", 1), ("z", 2), ("z", 1))


def heads_of(part):
    return HEADS[part:] + HEADS[:part]


def mark_of(part):
    bits = [(axis, 0) for head in heads_of(part) for axis in head] + list(TAIL)
    code = 0
    for axis, bit in bits:
        own = code_of(lax.axis_index(axis), lax.axis_index("side"), SIZES[axis])
        code = code * 2 + ((own >> bit) & 1)
    return code


def turned(value, axis, d):
    return jnp.concatenate(
        [lax.slice_in_dim(value, k ^ d, (k ^ d) + 1, axis=axis) for k in range(4)], axis=axis
    )


def halves(value):
    n = value.shape[0] // 2
    return value[:n], value[n:].astype(BF16)


def sum_weights(sends, keeps):
    sums = []
    for part in range(PARTS):
        keep, send = keeps[part], sends[part]
        for step in range(len(HEADS)):
            value = keep + trade(send, **heads_of(part)[step]).astype(F32)
            if step < len(HEADS) - 1:
                keep, send = halves(value)
        sums.append(value)
    value = jnp.stack(sums).reshape(PARTS, 4, 4, PIECE, 128)
    sent = value.astype(BF16)
    got = [trade(sent[:, d + 1], **flips) for d, flips in enumerate(PLANE_FOURS)]
    value = value[:, 0] + got[0].astype(F32) + got[1].astype(F32) + got[2].astype(F32)
    mine = value.astype(BF16)
    got = [
        turned(trade(mine, **flips), 1, d + 1).astype(F32) for d, flips in enumerate(TAIL_FOURS)
    ]
    return ((mine.astype(F32) + got[0]) + (got[1] + got[2])).astype(BF16)


def spread_weights(value):
    value = jnp.concatenate([value] + [trade(value, **flips) for flips in PLANE_FOURS], axis=1)
    pairs = []
    for part in range(PARTS):
        mine = value[part]
        heads = heads_of(part)[::-1]
        for head in heads[:-1]:
            mine = jnp.concatenate([mine, trade(mine, **head)], axis=0)
        pairs += [mine, trade(mine, **heads[-1])]
    return pairs


def on_device(node_table, owner, local_row, w_in, w_mid, w_out):
    side = lax.axis_index("side")
    yx = lax.axis_index("y") * NX + lax.axis_index("x")
    place = jnp.stack([yx, side] + [mark_of(part) for part in range(PARTS)]).astype(jnp.int32)
    table, weight_in, weight_mid, weight_out = node_table[0], w_in[0], w_mid[0], w_out[0]

    request, position = call(
        request_kernel,
        [((N_SHARD, 128), jnp.int32), ((1, TOK), jnp.int32)],
        [VMEM, VMEM],
    )(owner[0], local_row)
    incoming = exchange(request.reshape(N_SHARD, 1, 128), ALL).reshape(N_SHARD, 128)
    (picked,) = call(
        pick_kernel, [((N_SHARD * CAP, FEAT), BF16)], [VMEM, VMEM]
    )(incoming, table)
    arrived = exchange(picked.reshape(N_SHARD, CAP, FEAT), ALL).reshape(N_SHARD * CAP, FEAT)
    x, z1, z2, u, r, e = call(
        forward_kernel,
        [
            ((TOK, FEAT), BF16), ((TOK, HID), F32), ((TOK, HID), F32),
            ((TOK, EMB), F32), ((TOK, EMB), F32), ((TOK, EMB), BF16),
        ],
        [VMEM] * 5,
    )(position, arrived, weight_in, weight_mid, weight_out)

    partner = swap(e)
    mine, theirs = jnp.where(side == 0, e, partner), jnp.where(side == 0, partner, e)
    user_half = lax.dynamic_slice_in_dim(mine, side * HALF, HALF, 0)
    item_half = lax.dynamic_slice_in_dim(theirs, side * HALF, HALF, 0)
    items = spread(item_half, YX, NYX).reshape(ICOLS, EMB)
    own_users = user_half[None]
    for bit in USER_STEPS:
        own_users = jnp.concatenate([own_users, across(own_users, "z", bit)])
    own_users = own_users.reshape(UROWS, EMB)
    other_users = swap(own_users)

    row, col = call(
        sums_kernel, [((2 * NZ, 1, 128), F32), ((1, ICOLS), F32)], [VMEM] * 3
    )(own_users, other_users, items)
    col = total(spread(col.reshape(ICOLS // 128, 128), YX, NYX)).reshape(1, ICOLS)
    row = row.reshape(2, 2, 2, 2, 1, 128)
    row = row + jnp.flip(swap(row), 0)
    for k, bit in enumerate(USER_STEPS[::-1]):
        row = row + jnp.flip(across(row, "z", bit), k + 1)
    row = row.reshape(2 * NZ, 1, 128)

    grad_own, grad_other, grad_items = call(
        grad_kernel,
        [((UROWS, EMB), F32), ((UROWS, EMB), BF16), ((ICOLS, EMB), BF16)],
        [SMEM] + [VMEM] * 5,
        [pltpu.VMEM((CHUNK, ICOLS), F32), pltpu.VMEM((EMB, ICOLS), F32)],
    )(place, own_users, other_users, items, row, col)
    grad_items = total(exchange(grad_items.reshape(NYX, HALF, EMB), YX))
    grad_users = grad_own + swap(grad_other).astype(F32)
    for bit in USER_STEPS[::-1]:
        keep, send = halves(grad_users)
        grad_users = keep + across(send, "z", bit).astype(F32)
    kept = jnp.where(side == 0, grad_users, grad_items)
    sent = swap(jnp.where(side == 0, grad_items, grad_users))

    slots = (SLOTS, PIECE, 128)
    sums = call(
        backward_kernel,
        [(slots, BF16)] * PARTS + [(slots, F32)] * PARTS,
        [SMEM] + [VMEM] * 9,
        [pltpu.VMEM((WROWS, HID), F32)],
    )(place, kept, sent, x, z1, z2, u, r, weight_mid, weight_out)
    pairs = spread_weights(sum_weights(sums[:PARTS], sums[PARTS:]))
    grads = call(
        finish_kernel,
        [((FEAT, HID), F32), ((HID, HID), F32), ((HID, EMB), F32)],
        [SMEM] + [VMEM] * (2 * PARTS),
        [pltpu.VMEM((WROWS, HID), F32), pltpu.VMEM((HID, EMB), F32), pltpu.SemaphoreType.DMA((5,))],
        out_space=pl.ANY,
    )(place, *pairs)
    return tuple(g[None] for g in grads)


def solution(mesh):
    cube = Mesh(mesh.devices.reshape(2, NZ, NY, NX), ("side", "z", "y", "x"))
    rows = P("side", ALL, None)
    whole = P("side", None, None)
    return jax.shard_map(
        on_device,
        mesh=cube,
        in_specs=(rows, rows, P("side", ALL), whole, whole, whole),
        out_specs=(whole, whole, whole),
        check_vma=False,
    )
```

```python
import itertools
import math

import jax
import jax.numpy as jnp
from jax import lax
from jax.experimental import pallas as pl
from jax.experimental.pallas import tpu as pltpu
from jax.sharding import Mesh, PartitionSpec as P

NZ, NY, NX = 8, 4, 4
NYX = NY * NX
N_SHARD = NZ * NYX
CAP = 4
ROWS_DEV = 512
TOK = 256
FEAT, HID, EMB = 768, 1024, 128
TOKENS = N_SHARD * TOK
UROWS = NZ * TOK
ICOLS = NYX // 2 * TOK
QUART = 4 * TOK
EXP2_SCALE = 40.0 / math.log(2.0)
GRAD_SCALE = 40.0 * 0.5 / math.sqrt(TOKENS)
WROWS = FEAT + HID + EMB
PARTS = 3
PROWS = WROWS // PARTS
LANES = HID // 128
PIECE = PROWS * LANES // N_SHARD
BF16 = jnp.bfloat16
F32 = jnp.float32
VMEM = pl.BlockSpec(memory_space=pltpu.VMEM)
SMEM = pl.BlockSpec(memory_space=pltpu.SMEM)
ANY = pl.BlockSpec(memory_space=pl.ANY)


def call(kernel, outs, in_specs, scratch=(), mib=48, spaces=None):
    return pl.pallas_call(
        kernel,
        out_shape=[jax.ShapeDtypeStruct(s, d) for s, d in outs],
        in_specs=in_specs,
        out_specs=[pl.BlockSpec(memory_space=space) for space in spaces or [pltpu.VMEM] * len(outs)],
        scratch_shapes=list(scratch),
        compiler_params=pltpu.CompilerParams(vmem_limit_bytes=mib * 2**20),
    )


def dot(a, b, dims):
    return lax.dot_general(a, b, (dims, ((), ())), preferred_element_type=F32)


NN = ((1,), (0,))
NT = ((1,), (1,))
TN = ((0,), (0,))


def iota(shape, dim):
    return lax.broadcasted_iota(jnp.int32, shape, dim)


def begin(sources, targets, sems, first=0):
    copies = [
        pltpu.make_async_copy(source, target, sems.at[first + k])
        for k, (source, target) in enumerate(zip(sources, targets))
    ]
    for copy in copies:
        copy.start()
    return copies


def request_kernel(owner_ref, wanted_ref, request_ref, position_ref):
    own_row = jnp.broadcast_to(owner_ref[...].astype(F32), (TOK, TOK))
    own_col = own_row.T
    earlier = iota((TOK, TOK), 0) < iota((TOK, TOK), 1)
    same = jnp.where((own_col == own_row) & earlier, 1.0, 0.0)
    rank = jnp.sum(same, axis=0, keepdims=True)
    owners = own_row[0:1, :]
    position_ref[...] = (owners * CAP + rank).astype(jnp.int32)
    wanted = wanted_ref[...].astype(F32) + 1.0
    owner_hit = iota((N_SHARD, TOK), 0).astype(F32) == owners
    lanes = iota((N_SHARD, 128), 1)
    request = jnp.zeros((N_SHARD, 128), F32)
    for k in range(CAP):
        hit = jnp.where(owner_hit & (rank == float(k)), wanted, 0.0)
        slot = jnp.sum(hit, axis=1, keepdims=True)
        request = jnp.where(lanes == k, slot, request)
    request_ref[...] = request.astype(jnp.int32) - 1


def pick_kernel(incoming_ref, table_any, picked_ref, table_ref, sems):
    (copy,) = begin([table_any], [table_ref], sems)
    slots = N_SHARD * CAP
    spread = jnp.where(iota((slots, N_SHARD), 0) // CAP == iota((slots, N_SHARD), 1), 1.0, 0.0)
    listed = lax.dot_general(
        spread,
        incoming_ref[...].astype(F32),
        (NN, ((), ())),
        precision=lax.Precision.HIGHEST,
        preferred_element_type=F32,
    )
    mine = iota((slots, 128), 0) % CAP == iota((slots, 128), 1)
    row = jnp.sum(jnp.where(mine, listed, 0.0), axis=1, keepdims=True)
    hit = jnp.where(row == iota((slots, ROWS_DEV), 1).astype(F32), 1.0, 0.0).astype(BF16)
    copy.wait()
    picked_ref[...] = dot(hit, table_ref[...], NN).astype(BF16)


def silu(v):
    return v * (1.0 / (1.0 + jnp.exp(-v)))


def slope(v):
    q = 1.0 / (1.0 + jnp.exp(-v))
    return q * (1.0 + v * (1.0 - q))


def forward_kernel(
    position_ref, arrived_ref, w_in_any, w_mid_any, w_out_any,
    x_out, z1_out, z2_out, u_ref, r_ref, e_ref,
    w_in_ref, w_mid_ref, w_out_ref, x_ref, z1_ref, z2_ref, sems,
):
    loads = begin([w_in_any, w_mid_any, w_out_any], [w_in_ref, w_mid_ref, w_out_ref], sems)
    slots = N_SHARD * CAP
    hit = jnp.where(iota((slots, TOK), 0) == position_ref[...], 1.0, 0.0).astype(BF16)
    x = dot(hit, arrived_ref[...], TN).astype(BF16)
    x_ref[...] = x
    stores = begin([x_ref], [x_out], sems, 3)
    loads[0].wait()
    z1 = dot(x, w_in_ref[...], NN)
    z1_ref[...] = z1
    stores += begin([z1_ref], [z1_out], sems, 4)
    loads[1].wait()
    z2 = dot(silu(z1).astype(BF16), w_mid_ref[...], NN)
    z2_ref[...] = z2
    stores += begin([z2_ref], [z2_out], sems, 5)
    loads[2].wait()
    z3 = dot(silu(z2).astype(BF16), w_out_ref[...], NN)
    r = lax.rsqrt(jnp.sum(z3 * z3, axis=1, keepdims=True) + 1e-6)
    u = z3 * r
    u_ref[...] = u
    r_ref[...] = jnp.broadcast_to(r, (TOK, EMB))
    e_ref[...] = u.astype(BF16)
    for copy in stores:
        copy.wait()


CHUNK = TOK


def choose(side_ref, pieces):
    first = side_ref[0] == 0
    near, far, rest_near, rest_far, sent_near, sent_far = [piece[...] for piece in pieces]
    users = [jnp.where(first, near, sent_near), jnp.where(first, far, sent_far)]
    items = [jnp.where(first, sent_near, rest_near), jnp.where(first, sent_far, rest_far)]
    return users, jnp.concatenate(items, axis=0)


def rows_of(users, c):
    at = c * CHUNK % QUART
    return users[c * CHUNK // QUART][at:at + CHUNK, :]


def sums_kernel(side_ref, *refs):
    row_ref, col_ref = refs[6:]
    users, items = choose(side_ref, refs[:6])
    cols = jnp.zeros((8, ICOLS), F32)
    for c in range(NZ):
        expo = jnp.exp2(dot(rows_of(users, c), items, NT) * EXP2_SCALE)
        cols = cols + jnp.sum(expo.reshape(CHUNK // 8, 8, ICOLS), axis=0)
        folded = expo[:, 0:128]
        for k in range(1, ICOLS // 128):
            folded = folded + expo[:, k * 128:(k + 1) * 128]
        sums = jnp.sum(folded.T, axis=0, keepdims=True)
        for k in range(CHUNK // 128):
            row_ref[c * CHUNK // 128 + k] = sums[:, k * 128:(k + 1) * 128]
    sums = jnp.sum(cols, axis=0, keepdims=True)
    for k in range(ICOLS // 128):
        col_ref[k] = sums[:, k * 128:(k + 1) * 128]


def grad_kernel(side_ref, *refs):
    row_ref, col_ref, keep_ref, send_ref, away_ref, grad_ref, turned_ref = refs[6:]
    users, items = choose(side_ref, refs[:6])
    first = side_ref[0] == 0
    col_inv = 1.0 / jnp.concatenate([col_ref[k] for k in range(ICOLS // 128)], axis=1)
    for c in range(NZ):
        chunk = rows_of(users, c)
        scores = dot(chunk, items, NT)
        totals = [row_ref[c * CHUNK // 128 + k] for k in range(CHUNK // 128)]
        inv = jnp.broadcast_to(1.0 / jnp.concatenate(totals, axis=1), (128, CHUNK)).T[:, 0:1]
        grad_ref[...] = jnp.exp2(scores * EXP2_SCALE) * (inv + col_inv)
        if c == 0:
            own = jnp.where(first, 2.0, 0.0)
            eye = jnp.where(iota((TOK, TOK), 0) == iota((TOK, TOK), 1), own, 0.0)
            grad_ref[:, 0:TOK] = grad_ref[:, 0:TOK] - eye
        grad = grad_ref[...].astype(BF16)
        keep_ref[c * CHUNK:(c + 1) * CHUNK, :] = dot(grad, items, NN) * GRAD_SCALE
        term = dot(chunk, grad, TN)
        if c == 0:
            turned_ref[...] = term
        else:
            turned_ref[...] += term
    for c in range(NZ):
        rows = slice(c * CHUNK, (c + 1) * CHUNK)
        of_items = (turned_ref[:, rows].T * GRAD_SCALE).astype(BF16)
        away_ref[rows, :] = of_items
        send_ref[rows, :] = jnp.where(first, of_items, keep_ref[rows, :].astype(BF16))


def piece_at(part, slot, code):
    piece = slot ^ code
    row = pl.multiple_of(part * PROWS + lax.shift_right_logical(piece, 3) * PIECE, 8)
    lane = pl.multiple_of(lax.bitwise_and(piece, LANES - 1) * 128, 128)
    return pl.ds(row, PIECE), pl.ds(lane, 128)


SLOTS = N_SHARD // 2


def backward_kernel(
    place_ref, keep_ref, sent0_ref, sent1_ref, sent2_ref, u_ref, r_ref,
    z2_any, w_out_any, z1_any, w_mid_any, x_any, *rest,
):
    send_refs, keep_refs = rest[:PARTS], rest[PARTS:2 * PARTS]
    sums_ref, z2_ref, w_out_ref, z1_ref, w_mid_ref, x_ref, sems = rest[2 * PARTS:]
    loads = begin(
        [z2_any, w_out_any, z1_any, w_mid_any, x_any], [z2_ref, w_out_ref, z1_ref, w_mid_ref, x_ref], sems
    )
    g = keep_ref[...] + sent0_ref[...].astype(F32)
    g = g + sent1_ref[...].astype(F32) + sent2_ref[...].astype(F32)
    u = u_ref[...]
    along = jnp.sum(g * u, axis=1, keepdims=True)
    dz3 = ((g - u * along) * r_ref[...]).astype(BF16)
    loads[0].wait()
    z2 = z2_ref[...]
    h2 = silu(z2).astype(BF16)
    sums_ref[FEAT + HID:, :] = dot(dz3, h2, TN)
    loads[1].wait()
    dz2 = (dot(dz3, w_out_ref[...], NT) * slope(z2)).astype(BF16)
    loads[2].wait()
    z1 = z1_ref[...]
    h1 = silu(z1).astype(BF16)
    sums_ref[FEAT:FEAT + HID, :] = dot(h1, dz2, TN)
    loads[3].wait()
    dz1 = (dot(dz2, w_mid_ref[...], NT) * slope(z1)).astype(BF16)
    loads[4].wait()
    sums_ref[0:FEAT, :] = dot(x_ref[...], dz1, TN)
    for part in range(PARTS):
        code = place_ref[part]
        for slot in range(SLOTS):
            keep_refs[part][slot] = sums_ref[piece_at(part, slot, code)]
            send_refs[part][slot] = sums_ref[piece_at(part, SLOTS + slot, code)].astype(BF16)


def finish_kernel(place_ref, *rest):
    halves, outs = rest[:2 * PARTS], rest[2 * PARTS:2 * PARTS + 3]
    sums_ref, turned_ref, sems = rest[2 * PARTS + 3:]
    copies = []

    def send(source, out):
        copies.append(pltpu.make_async_copy(source, out, sems.at[len(copies)]))
        copies[-1].start()

    for part in range(PARTS):
        code = place_ref[part]
        for half in range(2):
            for slot in range(SLOTS):
                piece = halves[2 * part + half][slot].astype(F32)
                sums_ref[piece_at(part, half * SLOTS + slot, code)] = piece
        for k, (start, stop) in enumerate(((0, FEAT), (FEAT, FEAT + HID))):
            low, high = max(start, part * PROWS), min(stop, (part + 1) * PROWS)
            if low < high:
                send(sums_ref.at[low:high, :], outs[k].at[low - start:high - start, :])
    turned_ref[...] = sums_ref[FEAT + HID:, :].T
    send(turned_ref, outs[2])
    for copy in copies:
        copy.wait()


ALL = ("z", "y", "x")
AXES = ("side",) + ALL
SIZES = {"side": 2, "z": NZ, "y": NY, "x": NX}
PLACES = list(itertools.product(*(range(SIZES[axis]) for axis in AXES)))
NUMBERS = {place: k for k, place in enumerate(PLACES)}


def exchange(value, axes):
    return lax.all_to_all(value, axes, split_axis=0, concat_axis=0, tiled=True)


def swap(value):
    return lax.ppermute(value, "side", [(0, 1), (1, 0)])


def gray(i):
    return i ^ (i >> 1)


def across(value, *flips):
    pairs = []
    for place, number in NUMBERS.items():
        if flips[place[0]] is None:
            continue
        other = []
        for axis, i in zip(AXES, place):
            at = {gray(k): k for k in range(SIZES[axis])}
            other.append(at[gray(i) ^ flips[place[0]].get(axis, 0)])
        pairs.append((number, NUMBERS[tuple(other)]))
    return lax.ppermute(value, AXES, pairs)


def both(value, **flips):
    return across(value, flips, flips)


def code_of(i, side, n):
    return gray((i + side) % n)


def trade(value, **flips):
    pairs = []
    for place, number in NUMBERS.items():
        other = [place[0]]
        for axis, i in zip(ALL, place[1:]):
            n = SIZES[axis]
            at = {code_of(k, place[0], n): k for k in range(n)}
            other.append(at[code_of(i, place[0], n) ^ flips.get(axis, 0)])
        pairs.append((number, NUMBERS[tuple(other)]))
    return lax.ppermute(value, AXES, pairs)


PLANE_FOURS = (dict(y=2), dict(x=2), dict(x=2, y=2))
HEADS = (dict(x=1), dict(y=1), dict(z=1))
TAIL = (("x", 1), ("y", 1), ("z", 2), ("z", 1))


def heads_of(part):
    return HEADS[part:] + HEADS[:part]


def mark_of(part):
    bits = [(axis, 0) for head in heads_of(part) for axis in head] + list(TAIL)
    code = 0
    for axis, bit in bits:
        own = code_of(lax.axis_index(axis), lax.axis_index("side"), SIZES[axis])
        code = code * 2 + ((own >> bit) & 1)
    return code


def turned(value, axis, d):
    return jnp.concatenate(
        [lax.slice_in_dim(value, k ^ d, (k ^ d) + 1, axis=axis) for k in range(4)], axis=axis
    )


def halves(value):
    n = value.shape[0] // 2
    return value[:n], value[n:].astype(BF16)


def sum_weights(sends, keeps):
    sums = []
    for part in range(PARTS):
        keep, send = keeps[part], sends[part]
        for step in range(len(HEADS)):
            value = keep + trade(send, **heads_of(part)[step]).astype(F32)
            if step < len(HEADS) - 1:
                keep, send = halves(value)
        sums.append(value)
    value = jnp.stack(sums).reshape(PARTS, 4, 4, PIECE, 128)
    sent = value.astype(BF16)
    got = [trade(sent[:, d + 1], **flips) for d, flips in enumerate(PLANE_FOURS)]
    value = value[:, 0] + got[0].astype(F32) + got[1].astype(F32) + got[2].astype(F32)
    for bit, axis in ((4, 1), (2, 2)):
        mine = value.astype(BF16)
        got = trade(mine, z=bit).reshape(PARTS, 2, 2, PIECE, 128)
        mine = mine.astype(F32).reshape(PARTS, 2, 2, PIECE, 128)
        value = (mine + jnp.flip(got, axis).astype(F32)).reshape(PARTS, 4, PIECE, 128)
    return value.astype(BF16)


def spread_weights(value):
    value = jnp.concatenate([value] + [trade(value, **flips) for flips in PLANE_FOURS], axis=1)
    pairs = []
    for part in range(PARTS):
        mine = value[part]
        heads = heads_of(part)[::-1]
        for head in heads[:-1]:
            mine = jnp.concatenate([mine, trade(mine, **head)], axis=0)
        pairs += [mine, trade(mine, **heads[-1])]
    return pairs


FOURS = [({"z": 2 * d}, {"x": d}) for d in (1, 2, 3)]
ROW_FOURS = ({"side": 1}, {"z": 1}, {"side": 1, "z": 1})
COL_FOURS = ({"y": 1}, {"side": 1, "y": 2}, {"side": 1, "y": 3})


def sum_all(row, col):
    lanes = (TOK // 128, 1, 128)
    row, col = row.reshape((2, 4) + lanes), col.reshape((2, 4) + lanes)
    rows = [both(row, **flips) for flips in ROW_FOURS]
    cols = [turned(both(col, x=d), 1, d) for d in (1, 2, 3)]
    row = (row + rows[0]) + jnp.flip(rows[1] + rows[2], 0)
    col = (col + cols[0]) + (cols[1] + cols[2])
    rows = [turned(both(row, z=2 * d), 1, d) for d in (1, 2, 3)]
    cols = [both(col, **flips) for flips in COL_FOURS]
    row = (row + rows[0]) + (rows[1] + rows[2])
    col = (col + cols[1]) + jnp.flip(cols[0] + cols[2], 0)
    return row.reshape((-1, 1, 128)), col.reshape((-1, 1, 128))


def on_device(node_table, owner, local_row, w_in, w_mid, w_out):
    side = lax.axis_index("side").astype(jnp.int32)[None]
    place = jnp.stack([mark_of(part) for part in range(PARTS)]).astype(jnp.int32)
    table, weight_in, weight_mid, weight_out = node_table[0], w_in[0], w_mid[0], w_out[0]

    request, position = call(
        request_kernel,
        [((N_SHARD, 128), jnp.int32), ((1, TOK), jnp.int32)],
        [VMEM, VMEM],
    )(owner.reshape(1, TOK), local_row)
    incoming = exchange(request.reshape(N_SHARD, 1, 128), ALL).reshape(N_SHARD, 128)
    (picked,) = call(
        pick_kernel,
        [((N_SHARD * CAP, FEAT), BF16)],
        [VMEM, ANY],
        [pltpu.VMEM((ROWS_DEV, FEAT), BF16), pltpu.SemaphoreType.DMA((1,))],
    )(incoming, table)
    arrived = exchange(picked.reshape(N_SHARD, CAP, FEAT), ALL).reshape(N_SHARD * CAP, FEAT)
    weights = [pltpu.VMEM((FEAT, HID), BF16), pltpu.VMEM((HID, HID), BF16), pltpu.VMEM((HID, EMB), BF16)]
    saved = [pltpu.VMEM((TOK, FEAT), BF16), pltpu.VMEM((TOK, HID), F32), pltpu.VMEM((TOK, HID), F32)]
    x, z1, z2, u, r, e = call(
        forward_kernel,
        [
            ((TOK, FEAT), BF16), ((TOK, HID), F32), ((TOK, HID), F32),
            ((TOK, EMB), F32), ((TOK, EMB), F32), ((TOK, EMB), BF16),
        ],
        [VMEM, VMEM, ANY, ANY, ANY],
        weights + saved + [pltpu.SemaphoreType.DMA((6,))],
        spaces=[pltpu.HBM] * 3 + [pltpu.VMEM] * 3,
    )(position, arrived, weight_in, weight_mid, weight_out)

    near = jnp.concatenate([e] + [across(e, *flips) for flips in FOURS])
    far = across(near, {"z": 1}, {"y": 1})
    rest = [across(near, None, {"y": d}) for d in (2, 3)]
    pieces = [near, far] + rest + [swap(near), swap(far)]
    row, col = call(
        sums_kernel,
        [((UROWS // 128, 1, 128), F32), ((ICOLS // 128, 1, 128), F32)],
        [SMEM] + [VMEM] * 6,
    )(side, *pieces)
    row, col = sum_all(row, col)

    keep, send, away = call(
        grad_kernel,
        [((UROWS, EMB), F32), ((UROWS, EMB), BF16), ((ICOLS, EMB), BF16)],
        [SMEM] + [VMEM] * 8,
        [pltpu.VMEM((CHUNK, ICOLS), F32), pltpu.VMEM((EMB, ICOLS), F32)],
    )(side, *pieces, row, col)
    got = [across(away[(d - 2) * QUART:(d - 1) * QUART], None, {"y": d}) for d in (2, 3)]
    grad = jnp.where(side[0] == 0, keep, 0.0) + swap(send).astype(F32)
    got.append(across(grad[QUART:].astype(BF16), {"z": 1}, {"y": 1}))
    grad = grad[:QUART] + got[2].astype(F32) + got[0].astype(F32) + got[1].astype(F32)
    grad = grad.reshape(4, TOK, EMB)
    got = [across(grad[d + 1].astype(BF16), *flips) for d, flips in enumerate(FOURS)]

    slots = (SLOTS, PIECE, 128)
    sums = call(
        backward_kernel,
        [(slots, BF16)] * PARTS + [(slots, F32)] * PARTS,
        [SMEM] + [VMEM] * 6 + [ANY] * 5,
        [pltpu.VMEM((WROWS, HID), F32), saved[2], weights[2], saved[1], weights[1], saved[0]]
        + [pltpu.SemaphoreType.DMA((5,))],
    )(place, grad[0], *got, u, r, z2, weight_out, z1, weight_mid, x)
    pairs = spread_weights(sum_weights(sums[:PARTS], sums[PARTS:]))
    grads = call(
        finish_kernel,
        [((FEAT, HID), F32), ((HID, HID), F32), ((HID, EMB), F32)],
        [SMEM] + [VMEM] * (2 * PARTS),
        [pltpu.VMEM((WROWS, HID), F32), pltpu.VMEM((HID, EMB), F32), pltpu.SemaphoreType.DMA((5,))],
        spaces=[pl.ANY] * 3,
    )(place, *pairs)
    return tuple(g[None] for g in grads)


def solution(mesh):
    cube = Mesh(mesh.devices.reshape(2, NZ, NY, NX), ("side", "z", "y", "x"))
    rows = P("side", ALL, None)
    whole = P("side", None, None)
    return jax.shard_map(
        on_device,
        mesh=cube,
        in_specs=(rows, rows, P("side", ALL), whole, whole, whole),
        out_specs=(whole, whole, whole),
        check_vma=False,
    )
```

```python
import functools
import itertools
import math

import jax
import jax.numpy as jnp
from jax import lax
from jax.experimental import pallas as pl
from jax.experimental.pallas import tpu as pltpu
from jax.sharding import Mesh, PartitionSpec as P

NZ, NY, NX = 8, 4, 4
NYX = NY * NX
N_SHARD = NZ * NYX
CAP = 4
ROWS_DEV = 512
TOK = 256
FEAT, HID, EMB = 768, 1024, 128
SPLIT = 2
LINES = CAP * SPLIT
WIDTH = FEAT // SPLIT
TOKENS = N_SHARD * TOK
UROWS = NZ * TOK
ICOLS = NYX // 2 * TOK
QUART = 4 * TOK
EXP2_SCALE = 40.0 / math.log(2.0)
GRAD_SCALE = 40.0 * 0.5 / math.sqrt(TOKENS)
WROWS = FEAT + HID + EMB
PARTS = 3
PROWS = WROWS // PARTS
LANES = HID // 128
PIECE = PROWS * LANES // N_SHARD
BF16 = jnp.bfloat16
F32 = jnp.float32
VMEM = pl.BlockSpec(memory_space=pltpu.VMEM)
SMEM = pl.BlockSpec(memory_space=pltpu.SMEM)
ANY = pl.BlockSpec(memory_space=pl.ANY)


def call(kernel, outs, in_specs, scratch=(), mib=48, spaces=None):
    return pl.pallas_call(
        kernel,
        out_shape=[jax.ShapeDtypeStruct(s, d) for s, d in outs],
        in_specs=in_specs,
        out_specs=[pl.BlockSpec(memory_space=space) for space in spaces or [pltpu.VMEM] * len(outs)],
        scratch_shapes=list(scratch),
        compiler_params=pltpu.CompilerParams(vmem_limit_bytes=mib * 2**20),
    )


def dot(a, b, dims):
    return lax.dot_general(a, b, (dims, ((), ())), preferred_element_type=F32)


NN = ((1,), (0,))
NT = ((1,), (1,))
TN = ((0,), (0,))


def iota(shape, dim):
    return lax.broadcasted_iota(jnp.int32, shape, dim)


def begin(sources, targets, sems, first=0):
    copies = [
        pltpu.make_async_copy(source, target, sems.at[first + k])
        for k, (source, target) in enumerate(zip(sources, targets))
    ]
    for copy in copies:
        copy.start()
    return copies


def request_kernel(owner_ref, wanted_ref, request_ref, position_ref):
    own_row = jnp.broadcast_to(owner_ref[...].astype(F32), (TOK, TOK))
    own_col = own_row.T
    earlier = iota((TOK, TOK), 0) < iota((TOK, TOK), 1)
    same = jnp.where((own_col == own_row) & earlier, 1.0, 0.0)
    rank = jnp.sum(same, axis=0, keepdims=True)
    owners = own_row[0:1, :]
    position_ref[...] = (owners * LINES + rank).astype(jnp.int32)
    wanted = wanted_ref[...].astype(F32) + 1.0
    owner_hit = iota((N_SHARD, TOK), 0).astype(F32) == owners
    lanes = iota((N_SHARD, 128), 1)
    request = jnp.zeros((N_SHARD, 128), F32)
    for k in range(CAP):
        hit = jnp.where(owner_hit & (rank == float(k)), wanted, 0.0)
        slot = jnp.sum(hit, axis=1, keepdims=True)
        request = jnp.where(lanes == k, slot, request)
    request_ref[...] = request.astype(jnp.int32) - 1


def pick_kernel(incoming_ref, table_any, picked_ref, table_ref, sems):
    (copy,) = begin([table_any], [table_ref], sems)
    lines = N_SHARD * LINES
    spread = jnp.where(iota((lines, N_SHARD), 0) // LINES == iota((lines, N_SHARD), 1), 1.0, 0.0)
    listed = lax.dot_general(
        spread,
        incoming_ref[...].astype(F32),
        (NN, ((), ())),
        precision=lax.Precision.HIGHEST,
        preferred_element_type=F32,
    )
    mine = iota((lines, 128), 0) % CAP == iota((lines, 128), 1)
    row = jnp.sum(jnp.where(mine, listed, 0.0), axis=1, keepdims=True)
    hit = jnp.where(row == iota((lines, ROWS_DEV), 1).astype(F32), 1.0, 0.0).astype(BF16)
    half = iota((lines, WIDTH), 0) // CAP % SPLIT
    copy.wait()
    low = dot(hit, table_ref[:, 0:WIDTH], NN)
    high = dot(hit, table_ref[:, WIDTH:FEAT], NN)
    picked_ref[...] = jnp.where(half == 0, low, high).astype(BF16)


def finish(parts, half, place, halves, grads):
    n = len(parts)
    shapes = [(FEAT, HID), (HID, HID), (HID, EMB)]
    return pl.pallas_call(
        functools.partial(finish_kernel, parts, half),
        out_shape=[jax.ShapeDtypeStruct(shape, F32) for shape in shapes],
        in_specs=[SMEM] + [VMEM] * n + [ANY] * len(grads),
        out_specs=[ANY] * 3,
        scratch_shapes=[pltpu.VMEM((HROWS, HID), F32)] * n
        + [pltpu.VMEM((HID, EMB), F32), pltpu.SemaphoreType.DMA((2 * PARTS,))],
        input_output_aliases={1 + n + k: k for k in range(len(grads))},
        compiler_params=pltpu.CompilerParams(vmem_limit_bytes=16 * 2**20),
        cost_estimate=pl.CostEstimate(
            flops=0, transcendentals=0, bytes_accessed=n * SLOTS * PIECE * 128 * 6
        ),
    )(place, *halves, *grads)


def silu(v):
    return v * (1.0 / (1.0 + jnp.exp(-v)))


def slope(v):
    q = 1.0 / (1.0 + jnp.exp(-v))
    return q * (1.0 + v * (1.0 - q))


def forward_kernel(
    position_ref, arrived_any, w_in_any, w_mid_any, w_out_any,
    x_ref, u_ref, r_ref, e_ref, arrived_ref, w_in_ref, w_mid_ref, w_out_ref, sems,
):
    first = begin([arrived_any], [arrived_ref], sems, 3)
    loads = begin([w_in_any, w_mid_any, w_out_any], [w_in_ref, w_mid_ref, w_out_ref], sems)
    lines = iota((N_SHARD * LINES, TOK), 0)
    hits = [
        jnp.where(lines == position_ref[...] + h * CAP, 1.0, 0.0).astype(BF16) for h in range(SPLIT)
    ]
    first[0].wait()
    arrived = arrived_ref[...]
    x = jnp.concatenate([dot(hit, arrived, TN) for hit in hits], axis=1).astype(BF16)
    x_ref[...] = x
    loads[0].wait()
    z1 = dot(x, w_in_ref[...], NN)
    loads[1].wait()
    z2 = dot(silu(z1).astype(BF16), w_mid_ref[...], NN)
    loads[2].wait()
    z3 = dot(silu(z2).astype(BF16), w_out_ref[...], NN)
    r = lax.rsqrt(jnp.sum(z3 * z3, axis=1, keepdims=True) + 1e-6)
    u = z3 * r
    u_ref[...] = u
    r_ref[...] = jnp.broadcast_to(r, (TOK, EMB))
    e_ref[...] = u.astype(BF16)


CHUNK = TOK


def choose(side_ref, pieces):
    first = side_ref[0] == 0
    near, far, rest_near, rest_far, sent_near, sent_far = [piece[...] for piece in pieces]
    users = [jnp.where(first, near, sent_near), jnp.where(first, far, sent_far)]
    items = [jnp.where(first, sent_near, rest_near), jnp.where(first, sent_far, rest_far)]
    return users, jnp.concatenate(items, axis=0)


def rows_of(users, c):
    at = c * CHUNK % QUART
    return users[c * CHUNK // QUART][at:at + CHUNK, :]


LROWS = UROWS // 128


def sums_kernel(side_ref, *refs):
    keep_ref, send_ref = refs[6:]
    users, items = choose(side_ref, refs[:6])
    cols = jnp.zeros((8, ICOLS), F32)
    rows = []
    for c in range(NZ):
        expo = jnp.exp2(dot(rows_of(users, c), items, NT) * EXP2_SCALE)
        cols = cols + jnp.sum(expo.reshape(CHUNK // 8, 8, ICOLS), axis=0)
        folded = expo[:, 0:128]
        for k in range(1, ICOLS // 128):
            folded = folded + expo[:, k * 128:(k + 1) * 128]
        rows.append(jnp.sum(folded.T, axis=0, keepdims=True))
    rows = jnp.concatenate(rows, axis=1)
    cols = jnp.sum(cols, axis=0, keepdims=True)
    first = side_ref[0] == 0
    keep, send = jnp.where(first, rows, cols), jnp.where(first, cols, rows)
    for k in range(LROWS):
        keep_ref[k] = keep[:, k * 128:(k + 1) * 128]
        send_ref[k] = send[:, k * 128:(k + 1) * 128]


def grad_kernel(side_ref, *refs):
    total_ref, sent_ref, keep_ref, send_ref, away_ref, grad_ref, turned_ref = refs[6:]
    users, items = choose(side_ref, refs[:6])
    first = side_ref[0] == 0
    col = [jnp.where(first, sent_ref[k], total_ref[LROWS + k]) for k in range(LROWS)]
    col_inv = 1.0 / jnp.concatenate(col, axis=1)
    for c in range(NZ):
        chunk = rows_of(users, c)
        scores = dot(chunk, items, NT)
        places = range(c * CHUNK // 128, (c + 1) * CHUNK // 128)
        totals = [jnp.where(first, total_ref[k], sent_ref[k]) for k in places]
        inv = jnp.broadcast_to(1.0 / jnp.concatenate(totals, axis=1), (128, CHUNK)).T[:, 0:1]
        grad_ref[...] = jnp.exp2(scores * EXP2_SCALE) * (inv + col_inv)
        if c == 0:
            own = jnp.where(first, 2.0, 0.0)
            eye = jnp.where(iota((TOK, TOK), 0) == iota((TOK, TOK), 1), own, 0.0)
            grad_ref[:, 0:TOK] = grad_ref[:, 0:TOK] - eye
        grad = grad_ref[...].astype(BF16)
        keep_ref[c * CHUNK:(c + 1) * CHUNK, :] = dot(grad, items, NN) * GRAD_SCALE
        term = dot(chunk, grad, TN)
        if c == 0:
            turned_ref[...] = term
        else:
            turned_ref[...] += term
    for c in range(NZ):
        rows = slice(c * CHUNK, (c + 1) * CHUNK)
        of_items = (turned_ref[:, rows].T * GRAD_SCALE).astype(BF16)
        away_ref[rows, :] = of_items
        send_ref[rows, :] = jnp.where(first, of_items, keep_ref[rows, :].astype(BF16))


def piece_at(part, slot, code):
    piece = slot ^ code
    row = pl.multiple_of(part * PROWS + lax.shift_right_logical(piece, 3) * PIECE, 8)
    lane = pl.multiple_of(lax.bitwise_and(piece, LANES - 1) * 128, 128)
    return pl.ds(row, PIECE), pl.ds(lane, 128)


SLOTS = N_SHARD // 2


def slopes_kernel(
    x_ref, w_in_any, w_mid_any, h1_ref, h2_ref, s1_ref, s2_ref, w_in_ref, w_mid_ref, sems
):
    loads = begin([w_in_any, w_mid_any], [w_in_ref, w_mid_ref], sems)
    loads[0].wait()
    z1 = dot(x_ref[...], w_in_ref[...], NN)
    h1 = silu(z1).astype(BF16)
    h1_ref[...] = h1
    s1_ref[...] = slope(z1)
    loads[1].wait()
    z2 = dot(h1, w_mid_ref[...], NN)
    h2_ref[...] = silu(z2).astype(BF16)
    s2_ref[...] = slope(z2)


def backward_kernel(
    place_ref, keep_ref, sent0_ref, sent1_ref, sent2_ref, u_ref, r_ref,
    x_ref, h1_ref, h2_ref, s1_ref, s2_ref, w_mid_any, w_out_any, *rest,
):
    send_refs, keep_refs = rest[:PARTS], rest[PARTS:2 * PARTS]
    sums_ref, w_mid_ref, w_out_ref, sems = rest[2 * PARTS:]
    loads = begin([w_out_any, w_mid_any], [w_out_ref, w_mid_ref], sems)
    g = keep_ref[...] + sent0_ref[...].astype(F32)
    g = g + sent1_ref[...].astype(F32) + sent2_ref[...].astype(F32)
    u = u_ref[...]
    along = jnp.sum(g * u, axis=1, keepdims=True)
    dz3 = ((g - u * along) * r_ref[...]).astype(BF16)
    sums_ref[FEAT + HID:, :] = dot(dz3, h2_ref[...], TN)
    loads[0].wait()
    dz2 = (dot(dz3, w_out_ref[...], NT) * s2_ref[...]).astype(BF16)
    sums_ref[FEAT:FEAT + HID, :] = dot(h1_ref[...], dz2, TN)
    loads[1].wait()
    dz1 = (dot(dz2, w_mid_ref[...], NT) * s1_ref[...]).astype(BF16)
    sums_ref[0:FEAT, :] = dot(x_ref[...], dz1, TN)
    for part in range(PARTS):
        code = place_ref[part]
        for slot in range(SLOTS):
            keep_refs[part][slot] = sums_ref[piece_at(part, slot, code)].astype(BF16)
            send_refs[part][slot] = sums_ref[piece_at(part, SLOTS + slot, code)].astype(BF16)


HROWS = PROWS // 2
GRADS = ((0, FEAT), (FEAT, FEAT + HID), (FEAT + HID, WROWS))


def finish_kernel(parts, half, place_ref, *rest):
    n = len(parts)
    refs, rest = rest[:n], rest[n:] if half == 0 else rest[n + 3:]
    outs, rows_refs, turned_ref, sems = rest[:3], rest[3:3 + n], rest[3 + n], rest[4 + n]

    def copies_of(part, k, rows_ref, turn=True):
        base = part * PROWS + k * HROWS
        copies = []
        for out, (start, stop) in zip(outs, GRADS):
            low, high = max(start, base), min(stop, base + HROWS)
            if low >= high:
                continue
            source = rows_ref.at[low - base:high - base, :]
            target = out.at[low - start:high - start, :]
            if start == GRADS[2][0]:
                if turn:
                    turned_ref[...] = rows_ref[low - base:high - base, :].T
                source, target = turned_ref, out
            copies.append(pltpu.make_async_copy(source, target, sems.at[2 * part + len(copies)]))
        return copies

    for part, ref, rows_ref in zip(parts, refs, rows_refs):
        code = place_ref[part]
        for slot in range(SLOTS):
            piece = lax.bitwise_and(slot ^ code, SLOTS - 1)
            row = pl.multiple_of(lax.shift_right_logical(piece, 3) * PIECE, 8)
            lane = pl.multiple_of(lax.bitwise_and(piece, LANES - 1) * 128, 128)
            rows_ref[pl.ds(row, PIECE), pl.ds(lane, 128)] = ref[slot].astype(F32)
        for k in range(2):
            @pl.when((lax.shift_right_logical(code, 6) ^ half) == k)
            def _():
                for copy in copies_of(part, k, rows_ref):
                    copy.start()
    for part, rows_ref in zip(parts, rows_refs):
        for k in range(2):
            @pl.when((lax.shift_right_logical(place_ref[part], 6) ^ half) == k)
            def _():
                for copy in copies_of(part, k, rows_ref, False):
                    copy.wait()


ALL = ("z", "y", "x")
AXES = ("side",) + ALL
SIZES = {"side": 2, "z": NZ, "y": NY, "x": NX}
PLACES = list(itertools.product(*(range(SIZES[axis]) for axis in AXES)))
NUMBERS = {place: k for k, place in enumerate(PLACES)}


def exchange(value, axes):
    return lax.all_to_all(value, axes, split_axis=0, concat_axis=0, tiled=True)


def swap(value):
    return lax.ppermute(value, "side", [(0, 1), (1, 0)])


def gray(i):
    return i ^ (i >> 1)


def across(value, *flips):
    pairs = []
    for place, number in NUMBERS.items():
        if flips[place[0]] is None:
            continue
        other = []
        for axis, i in zip(AXES, place):
            at = {gray(k): k for k in range(SIZES[axis])}
            other.append(at[gray(i) ^ flips[place[0]].get(axis, 0)])
        pairs.append((number, NUMBERS[tuple(other)]))
    return lax.ppermute(value, AXES, pairs)


def both(value, **flips):
    return across(value, flips, flips)


def code_of(i, side, n):
    return gray((i + side) % n)


def trade(value, **flips):
    pairs = []
    for place, number in NUMBERS.items():
        other = [place[0]]
        for axis, i in zip(ALL, place[1:]):
            n = SIZES[axis]
            at = {code_of(k, place[0], n): k for k in range(n)}
            other.append(at[code_of(i, place[0], n) ^ flips.get(axis, 0)])
        pairs.append((number, NUMBERS[tuple(other)]))
    return lax.ppermute(value, AXES, pairs)


PLANE_FOURS = (dict(y=2), dict(x=2), dict(x=2, y=2))
HEADS = (dict(x=1), dict(y=1), dict(z=1))
TAIL = (("x", 1), ("y", 1), ("z", 2), ("z", 1))


def heads_of(part):
    return HEADS[part:] + HEADS[:part]


def mark_of(part):
    bits = [(axis, 0) for head in heads_of(part) for axis in head] + list(TAIL)
    code = 0
    for axis, bit in bits:
        own = code_of(lax.axis_index(axis), lax.axis_index("side"), SIZES[axis])
        code = code * 2 + ((own >> bit) & 1)
    return code


def turned(value, axis, d):
    return jnp.concatenate(
        [lax.slice_in_dim(value, k ^ d, (k ^ d) + 1, axis=axis) for k in range(4)], axis=axis
    )


def halves(value):
    n = value.shape[0] // 2
    return value[:n], value[n:].astype(BF16)


def sum_weights(sends, keeps):
    sums = []
    for part in range(PARTS):
        keep, send = keeps[part], sends[part]
        for step in range(len(HEADS)):
            value = keep.astype(F32) + trade(send, **heads_of(part)[step]).astype(F32)
            if step < len(HEADS) - 1:
                keep, send = halves(value)
        sums.append(value)
    value = jnp.stack(sums).reshape(PARTS, 4, 4, PIECE, 128)
    sent = value.astype(BF16)
    got = [trade(sent[:, d + 1], **flips) for d, flips in enumerate(PLANE_FOURS)]
    value = value[:, 0] + got[0].astype(F32) + got[1].astype(F32) + got[2].astype(F32)
    for bit, axis in ((4, 1), (2, 2)):
        mine = value.astype(BF16)
        got = trade(mine, z=bit).reshape(PARTS, 2, 2, PIECE, 128)
        mine = mine.astype(F32).reshape(PARTS, 2, 2, PIECE, 128)
        value = (mine + jnp.flip(got, axis).astype(F32)).reshape(PARTS, 4, PIECE, 128)
    return value.astype(BF16)


def spread_weights(value):
    value = jnp.concatenate([value] + [trade(value, **flips) for flips in PLANE_FOURS], axis=1)
    pairs = []
    for part in range(PARTS):
        mine = value[part]
        heads = heads_of(part)[::-1]
        for head in heads[:-1]:
            mine = jnp.concatenate([mine, trade(mine, **head)], axis=0)
        pairs += [mine, trade(mine, **heads[-1])]
    return pairs


FOURS = [({"z": 2 * d}, {"x": d}) for d in (1, 2, 3)]


def sum_all(keep, send, side):
    sent = swap(send)
    value = jnp.concatenate([sent + jnp.where(side == 0, keep, 0.0), keep])
    value = value.reshape(4, 4, TOK // 128, 1, 128)
    got = [turned(across(value, *flips), 1, d + 1) for d, flips in enumerate(FOURS)]
    value = (value + got[0]) + (got[1] + got[2])
    got = [turned(across(value, {"z": 1} if d == 1 else None, {"y": d}), 0, d) for d in (1, 2, 3)]
    value = ((value + got[0]) + (got[1] + got[2])).reshape(2 * LROWS, 1, 128)
    return value, swap(value[:LROWS])


def on_device(node_table, owner, local_row, w_in, w_mid, w_out):
    side = lax.axis_index("side").astype(jnp.int32)[None]
    place = jnp.stack([mark_of(part) for part in range(PARTS)]).astype(jnp.int32)
    table, weight_in, weight_mid, weight_out = node_table[0], w_in[0], w_mid[0], w_out[0]

    request, position = call(
        request_kernel,
        [((N_SHARD, 128), jnp.int32), ((1, TOK), jnp.int32)],
        [VMEM, VMEM],
    )(owner.reshape(1, TOK), local_row)
    incoming = exchange(request.reshape(N_SHARD, 1, 128), ALL).reshape(N_SHARD, 128)
    (picked,) = call(
        pick_kernel,
        [((N_SHARD * LINES, WIDTH), BF16)],
        [VMEM, ANY],
        [pltpu.VMEM((ROWS_DEV, FEAT), BF16), pltpu.SemaphoreType.DMA((1,))],
        mib=48,
    )(incoming, table)
    arrived = exchange(picked.reshape(N_SHARD, LINES, WIDTH), ALL).reshape(N_SHARD * LINES, WIDTH)
    weights = [pltpu.VMEM((FEAT, HID), BF16), pltpu.VMEM((HID, HID), BF16), pltpu.VMEM((HID, EMB), BF16)]
    x, u, r, e = call(
        forward_kernel,
        [
            ((TOK, FEAT), BF16), ((TOK, EMB), F32), ((TOK, EMB), F32), ((TOK, EMB), BF16),
        ],
        [VMEM, ANY, ANY, ANY, ANY],
        [pltpu.VMEM((N_SHARD * LINES, WIDTH), BF16)] + weights + [pltpu.SemaphoreType.DMA((4,))],
        mib=63,
    )(position, arrived, weight_in, weight_mid, weight_out)

    near = jnp.concatenate([e] + [across(e, *flips) for flips in FOURS])
    far = across(near, {"z": 1}, {"y": 1})
    rest = [across(near, None, {"y": d}) for d in (2, 3)]
    pieces = [near, far] + rest + [swap(near), swap(far)]
    sums = call(
        sums_kernel, [((LROWS, 1, 128), F32)] * 2, [SMEM] + [VMEM] * 6, mib=32
    )(side, *pieces)
    sums = sum_all(*sums, side[0])

    keep, send, away = call(
        grad_kernel,
        [((UROWS, EMB), F32), ((UROWS, EMB), BF16), ((ICOLS, EMB), BF16)],
        [SMEM] + [VMEM] * 8,
        [pltpu.VMEM((CHUNK, ICOLS), F32), pltpu.VMEM((EMB, ICOLS), F32)],
        mib=32,
    )(side, *pieces, *sums)
    got = [across(away[(d - 2) * QUART:(d - 1) * QUART], None, {"y": d}) for d in (2, 3)]
    grad = jnp.where(side[0] == 0, keep, 0.0) + swap(send).astype(F32)
    got.append(across(grad[QUART:].astype(BF16), {"z": 1}, {"y": 1}))
    grad = grad[:QUART] + got[2].astype(F32) + got[0].astype(F32) + got[1].astype(F32)
    grad = grad.reshape(4, TOK, EMB)
    got = [across(grad[d + 1].astype(BF16), *flips) for d, flips in enumerate(FOURS)]

    wide = (TOK, HID)
    slopes = call(
        slopes_kernel,
        [(wide, BF16), (wide, BF16), (wide, F32), (wide, F32)],
        [VMEM, ANY, ANY],
        weights[:2] + [pltpu.SemaphoreType.DMA((2,))],
        mib=16,
    )(x, weight_in, weight_mid)
    slots = (SLOTS, PIECE, 128)
    sums = call(
        backward_kernel,
        [(slots, BF16)] * (2 * PARTS),
        [SMEM] + [VMEM] * 11 + [ANY] * 2,
        [pltpu.VMEM((WROWS, HID), F32)] + weights[1:] + [pltpu.SemaphoreType.DMA((2,))],
        mib=32,
    )(place, grad[0], *got, u, r, x, *slopes, weight_mid, weight_out)
    pairs = spread_weights(sum_weights(sums[:PARTS], sums[PARTS:]))
    grads = finish(tuple(range(PARTS)), 0, place, pairs[0::2], ())
    grads = finish(tuple(range(PARTS)), 1, place, pairs[1::2], grads)
    return tuple(g[None] for g in grads)


def solution(mesh):
    cube = Mesh(mesh.devices.reshape(2, NZ, NY, NX), ("side", "z", "y", "x"))
    rows = P("side", ALL, None)
    whole = P("side", None, None)
    return jax.shard_map(
        on_device,
        mesh=cube,
        in_specs=(rows, rows, P("side", ALL), whole, whole, whole),
        out_specs=(whole, whole, whole),
        check_vma=False,
    )
```

```python
import functools
import itertools
import math

import jax
import jax.numpy as jnp
from jax import lax
from jax.experimental import pallas as pl
from jax.experimental.pallas import tpu as pltpu
from jax.sharding import Mesh, PartitionSpec as P

NZ, NY, NX = 8, 4, 4
NYX = NY * NX
N_SHARD = NZ * NYX
CAP = 4
ROWS_DEV = 512
TOK = 256
FEAT, HID, EMB = 768, 1024, 128
SPLIT = 2
LINES = CAP * SPLIT
WIDTH = FEAT // SPLIT
TOKENS = N_SHARD * TOK
UROWS = NZ * TOK
ICOLS = NYX // 2 * TOK
QUART = 4 * TOK
EXP2_SCALE = 40.0 / math.log(2.0)
GRAD_SCALE = 40.0 * 0.5 / math.sqrt(TOKENS)
WROWS = FEAT + HID + EMB
PARTS = 3
PROWS = WROWS // PARTS
LANES = HID // 128
PIECE = PROWS * LANES // N_SHARD
BF16 = jnp.bfloat16
F32 = jnp.float32
VMEM = pl.BlockSpec(memory_space=pltpu.VMEM)
SMEM = pl.BlockSpec(memory_space=pltpu.SMEM)
ANY = pl.BlockSpec(memory_space=pl.ANY)


def call(kernel, outs, in_specs, scratch=(), mib=48, spaces=None):
    return pl.pallas_call(
        kernel,
        out_shape=[jax.ShapeDtypeStruct(s, d) for s, d in outs],
        in_specs=in_specs,
        out_specs=[pl.BlockSpec(memory_space=space) for space in spaces or [pltpu.VMEM] * len(outs)],
        scratch_shapes=list(scratch),
        compiler_params=pltpu.CompilerParams(vmem_limit_bytes=mib * 2**20),
    )


def dot(a, b, dims):
    return lax.dot_general(a, b, (dims, ((), ())), preferred_element_type=F32)


NN = ((1,), (0,))
NT = ((1,), (1,))
TN = ((0,), (0,))


def iota(shape, dim):
    return lax.broadcasted_iota(jnp.int32, shape, dim)


def begin(sources, targets, sems, first=0):
    copies = [
        pltpu.make_async_copy(source, target, sems.at[first + k])
        for k, (source, target) in enumerate(zip(sources, targets))
    ]
    for copy in copies:
        copy.start()
    return copies


def request_kernel(owner_any, wanted_any, request_ref, position_ref, owner_ref, wanted_ref, sems):
    for copy in begin([owner_any, wanted_any], [owner_ref, wanted_ref], sems):
        copy.wait()
    own_row = jnp.broadcast_to(owner_ref[...].astype(F32), (TOK, TOK))
    own_col = own_row.T
    earlier = iota((TOK, TOK), 0) < iota((TOK, TOK), 1)
    same = jnp.where((own_col == own_row) & earlier, 1.0, 0.0)
    rank = jnp.sum(same, axis=0, keepdims=True)
    owners = own_row[0:1, :]
    position_ref[...] = (owners * LINES + rank * SPLIT).astype(jnp.int32)
    wanted = wanted_ref[...].astype(F32) + 1.0
    owner_hit = iota((N_SHARD, TOK), 0).astype(F32) == owners
    lanes = iota((N_SHARD, 128), 1)
    request = jnp.zeros((N_SHARD, 128), F32)
    for k in range(CAP):
        hit = jnp.where(owner_hit & (rank == float(k)), wanted, 0.0)
        slot = jnp.sum(hit, axis=1, keepdims=True)
        request = jnp.where(lanes == k, slot, request)
    request_ref[...] = request.astype(jnp.int32) - 1


def pick_kernel(incoming_ref, table_any, picked_ref, table_ref, lines_ref, sems):
    (copy,) = begin([table_any], [table_ref], sems)
    slots = N_SHARD * CAP
    spread = jnp.where(iota((slots, N_SHARD), 0) // CAP == iota((slots, N_SHARD), 1), 1.0, 0.0)
    listed = lax.dot_general(
        spread,
        incoming_ref[...].astype(F32),
        (NN, ((), ())),
        precision=lax.Precision.HIGHEST,
        preferred_element_type=F32,
    )
    mine = iota((slots, 128), 0) % CAP == iota((slots, 128), 1)
    row = jnp.sum(jnp.where(mine, listed, 0.0), axis=1, keepdims=True)
    hit = jnp.where(row == iota((slots, ROWS_DEV), 1).astype(F32), 1.0, 0.0).astype(BF16)
    copy.wait()
    for h in range(SPLIT):
        for k in range(WIDTH // 128):
            lanes = slice(h * WIDTH + k * 128, h * WIDTH + (k + 1) * 128)
            lines_ref[k, pl.ds(h, slots, stride=SPLIT), :] = dot(hit, table_ref[:, lanes], NN)
    for k in range(WIDTH // 128):
        picked_ref[:, k * 128:(k + 1) * 128] = lines_ref[k].astype(BF16)


def finish(parts, half, place, halves, grads):
    n = len(parts)
    shapes = [(FEAT, HID), (HID, HID), (HID, EMB)]
    return pl.pallas_call(
        functools.partial(finish_kernel, parts, half),
        out_shape=[jax.ShapeDtypeStruct(shape, F32) for shape in shapes],
        in_specs=[SMEM] + [VMEM] * n + [ANY] * len(grads),
        out_specs=[ANY] * 3,
        scratch_shapes=[pltpu.VMEM((HROWS, HID), F32)] * n
        + [pltpu.VMEM((HID, EMB), F32), pltpu.SemaphoreType.DMA((2 * PARTS,))],
        input_output_aliases={1 + n + k: k for k in range(len(grads))},
        compiler_params=pltpu.CompilerParams(vmem_limit_bytes=16 * 2**20),
        cost_estimate=pl.CostEstimate(
            flops=0, transcendentals=0, bytes_accessed=n * SLOTS * PIECE * 128 * 6
        ),
    )(place, *halves, *grads)


def silu(v):
    return v * (1.0 / (1.0 + jnp.exp(-v)))


def slope(v):
    q = 1.0 / (1.0 + jnp.exp(-v))
    return q * (1.0 + v * (1.0 - q))


def forward_kernel(
    position_ref, arrived_any, w_in_any, w_mid_any, w_out_any,
    x_ref, u_ref, r_ref, e_ref, arrived_ref, w_in_ref, w_mid_ref, w_out_ref, sems,
):
    first = begin([arrived_any], [arrived_ref], sems, 3)
    loads = begin([w_in_any, w_mid_any, w_out_any], [w_in_ref, w_mid_ref, w_out_ref], sems)
    lines = iota((N_SHARD * LINES, TOK), 0)
    hits = [
        jnp.where(lines == position_ref[...] + h, 1.0, 0.0).astype(BF16) for h in range(SPLIT)
    ]
    first[0].wait()
    arrived = arrived_ref[...]
    x = jnp.concatenate([dot(hit, arrived, TN) for hit in hits], axis=1).astype(BF16)
    x_ref[...] = x
    loads[0].wait()
    z1 = dot(x, w_in_ref[...], NN)
    loads[1].wait()
    z2 = dot(silu(z1).astype(BF16), w_mid_ref[...], NN)
    loads[2].wait()
    z3 = dot(silu(z2).astype(BF16), w_out_ref[...], NN)
    r = lax.rsqrt(jnp.sum(z3 * z3, axis=1, keepdims=True) + 1e-6)
    u = z3 * r
    u_ref[...] = u
    r_ref[...] = jnp.broadcast_to(r, (TOK, EMB))
    e_ref[...] = u.astype(BF16)


CHUNK = TOK


def choose(side_ref, pieces):
    first = side_ref[0] == 0
    near, far, rest_near, rest_far, sent_near, sent_far = [piece[...] for piece in pieces]
    users = [jnp.where(first, near, sent_near), jnp.where(first, far, sent_far)]
    items = [jnp.where(first, sent_near, rest_near), jnp.where(first, sent_far, rest_far)]
    return users, jnp.concatenate(items, axis=0)


def rows_of(users, c):
    at = c * CHUNK % QUART
    return users[c * CHUNK // QUART][at:at + CHUNK, :]


LROWS = UROWS // 128


def sums_kernel(side_ref, *refs):
    keep_ref, send_ref = refs[6:]
    users, items = choose(side_ref, refs[:6])
    cols = jnp.zeros((8, ICOLS), F32)
    rows = []
    for c in range(NZ):
        expo = jnp.exp2(dot(rows_of(users, c), items, NT) * EXP2_SCALE)
        cols = cols + jnp.sum(expo.reshape(CHUNK // 8, 8, ICOLS), axis=0)
        folded = expo[:, 0:128]
        for k in range(1, ICOLS // 128):
            folded = folded + expo[:, k * 128:(k + 1) * 128]
        rows.append(jnp.sum(folded.T, axis=0, keepdims=True))
    rows = jnp.concatenate(rows, axis=1)
    cols = jnp.sum(cols, axis=0, keepdims=True)
    first = side_ref[0] == 0
    keep, send = jnp.where(first, rows, cols), jnp.where(first, cols, rows)
    for k in range(LROWS):
        keep_ref[k] = keep[:, k * 128:(k + 1) * 128]
        send_ref[k] = send[:, k * 128:(k + 1) * 128]


def grad_kernel(side_ref, *refs):
    total_ref, sent_ref, keep_ref, send_ref, away_ref, grad_ref, turned_ref = refs[6:]
    users, items = choose(side_ref, refs[:6])
    first = side_ref[0] == 0
    col = [jnp.where(first, sent_ref[k], total_ref[LROWS + k]) for k in range(LROWS)]
    col_inv = 1.0 / jnp.concatenate(col, axis=1)
    for c in range(NZ):
        chunk = rows_of(users, c)
        scores = dot(chunk, items, NT)
        places = range(c * CHUNK // 128, (c + 1) * CHUNK // 128)
        totals = [jnp.where(first, total_ref[k], sent_ref[k]) for k in places]
        inv = jnp.broadcast_to(1.0 / jnp.concatenate(totals, axis=1), (128, CHUNK)).T[:, 0:1]
        grad_ref[...] = jnp.exp2(scores * EXP2_SCALE) * (inv + col_inv)
        if c == 0:
            own = jnp.where(first, 2.0, 0.0)
            eye = jnp.where(iota((TOK, TOK), 0) == iota((TOK, TOK), 1), own, 0.0)
            grad_ref[:, 0:TOK] = grad_ref[:, 0:TOK] - eye
        grad = grad_ref[...].astype(BF16)
        keep_ref[c * CHUNK:(c + 1) * CHUNK, :] = dot(grad, items, NN) * GRAD_SCALE
        term = dot(chunk, grad, TN)
        if c == 0:
            turned_ref[...] = term
        else:
            turned_ref[...] += term
    for c in range(NZ):
        rows = slice(c * CHUNK, (c + 1) * CHUNK)
        of_items = (turned_ref[:, rows].T * GRAD_SCALE).astype(BF16)
        away_ref[rows, :] = of_items
        send_ref[rows, :] = jnp.where(first, of_items, keep_ref[rows, :].astype(BF16))


def piece_at(part, slot, code):
    piece = slot ^ code
    row = pl.multiple_of(part * PROWS + lax.shift_right_logical(piece, 3) * PIECE, 8)
    lane = pl.multiple_of(lax.bitwise_and(piece, LANES - 1) * 128, 128)
    return pl.ds(row, PIECE), pl.ds(lane, 128)


SLOTS = N_SHARD // 2


def slopes_kernel(
    x_ref, w_in_any, w_mid_any, h1_ref, h2_ref, s1_ref, s2_ref, w_in_ref, w_mid_ref, sems
):
    loads = begin([w_in_any, w_mid_any], [w_in_ref, w_mid_ref], sems)
    loads[0].wait()
    z1 = dot(x_ref[...], w_in_ref[...], NN)
    h1 = silu(z1).astype(BF16)
    h1_ref[...] = h1
    s1_ref[...] = slope(z1)
    loads[1].wait()
    z2 = dot(h1, w_mid_ref[...], NN)
    h2_ref[...] = silu(z2).astype(BF16)
    s2_ref[...] = slope(z2)


def backward_kernel(
    place_ref, keep_ref, sent0_ref, sent1_ref, sent2_ref, u_ref, r_ref,
    x_ref, h1_ref, h2_ref, s1_ref, s2_ref, w_mid_any, w_out_any, *rest,
):
    send_refs, keep_refs = rest[:PARTS], rest[PARTS:2 * PARTS]
    sums_ref, w_mid_ref, w_out_ref, sems = rest[2 * PARTS:]
    loads = begin([w_out_any, w_mid_any], [w_out_ref, w_mid_ref], sems)
    g = keep_ref[...] + sent0_ref[...].astype(F32)
    g = g + sent1_ref[...].astype(F32) + sent2_ref[...].astype(F32)
    u = u_ref[...]
    along = jnp.sum(g * u, axis=1, keepdims=True)
    dz3 = ((g - u * along) * r_ref[...]).astype(BF16)
    sums_ref[FEAT + HID:, :] = dot(dz3, h2_ref[...], TN)
    loads[0].wait()
    dz2 = (dot(dz3, w_out_ref[...], NT) * s2_ref[...]).astype(BF16)
    sums_ref[FEAT:FEAT + HID, :] = dot(h1_ref[...], dz2, TN)
    loads[1].wait()
    dz1 = (dot(dz2, w_mid_ref[...], NT) * s1_ref[...]).astype(BF16)
    sums_ref[0:FEAT, :] = dot(x_ref[...], dz1, TN)
    for part in range(PARTS):
        code = place_ref[part]
        for slot in range(SLOTS):
            keep_refs[part][slot] = sums_ref[piece_at(part, slot, code)].astype(BF16)
            send_refs[part][slot] = sums_ref[piece_at(part, SLOTS + slot, code)].astype(BF16)


HROWS = PROWS // 2
GRADS = ((0, FEAT), (FEAT, FEAT + HID), (FEAT + HID, WROWS))


def finish_kernel(parts, half, place_ref, *rest):
    n = len(parts)
    refs, rest = rest[:n], rest[n:] if half == 0 else rest[n + 3:]
    outs, rows_refs, turned_ref, sems = rest[:3], rest[3:3 + n], rest[3 + n], rest[4 + n]

    def copies_of(part, k, rows_ref, turn=True):
        base = part * PROWS + k * HROWS
        copies = []
        for out, (start, stop) in zip(outs, GRADS):
            low, high = max(start, base), min(stop, base + HROWS)
            if low >= high:
                continue
            source = rows_ref.at[low - base:high - base, :]
            target = out.at[low - start:high - start, :]
            if start == GRADS[2][0]:
                if turn:
                    turned_ref[...] = rows_ref[low - base:high - base, :].T
                source, target = turned_ref, out
            copies.append(pltpu.make_async_copy(source, target, sems.at[2 * part + len(copies)]))
        return copies

    for part, ref, rows_ref in zip(parts, refs, rows_refs):
        code = place_ref[part]
        for slot in range(SLOTS):
            piece = lax.bitwise_and(slot ^ code, SLOTS - 1)
            row = pl.multiple_of(lax.shift_right_logical(piece, 3) * PIECE, 8)
            lane = pl.multiple_of(lax.bitwise_and(piece, LANES - 1) * 128, 128)
            rows_ref[pl.ds(row, PIECE), pl.ds(lane, 128)] = ref[slot].astype(F32)
        for k in range(2):
            @pl.when((lax.shift_right_logical(code, 6) ^ half) == k)
            def _():
                for copy in copies_of(part, k, rows_ref):
                    copy.start()
    for part, rows_ref in zip(parts, rows_refs):
        for k in range(2):
            @pl.when((lax.shift_right_logical(place_ref[part], 6) ^ half) == k)
            def _():
                for copy in copies_of(part, k, rows_ref, False):
                    copy.wait()


ALL = ("z", "y", "x")
AXES = ("side",) + ALL
SIZES = {"side": 2, "z": NZ, "y": NY, "x": NX}
PLACES = list(itertools.product(*(range(SIZES[axis]) for axis in AXES)))
NUMBERS = {place: k for k, place in enumerate(PLACES)}


def exchange(value, axes):
    return lax.all_to_all(value, axes, split_axis=0, concat_axis=0, tiled=True)


def swap(value):
    return lax.ppermute(value, "side", [(0, 1), (1, 0)])


def gray(i):
    return i ^ (i >> 1)


def across(value, *flips):
    pairs = []
    for place, number in NUMBERS.items():
        if flips[place[0]] is None:
            continue
        other = []
        for axis, i in zip(AXES, place):
            at = {gray(k): k for k in range(SIZES[axis])}
            other.append(at[gray(i) ^ flips[place[0]].get(axis, 0)])
        pairs.append((number, NUMBERS[tuple(other)]))
    return lax.ppermute(value, AXES, pairs)


def both(value, **flips):
    return across(value, flips, flips)


def code_of(i, side, n):
    return gray((i + side) % n)


def trade(value, **flips):
    pairs = []
    for place, number in NUMBERS.items():
        other = [place[0]]
        for axis, i in zip(ALL, place[1:]):
            n = SIZES[axis]
            at = {code_of(k, place[0], n): k for k in range(n)}
            other.append(at[code_of(i, place[0], n) ^ flips.get(axis, 0)])
        pairs.append((number, NUMBERS[tuple(other)]))
    return lax.ppermute(value, AXES, pairs)


PLANE_FOURS = (dict(y=2), dict(x=2), dict(x=2, y=2))
HEADS = (dict(x=1), dict(y=1), dict(z=1))
TAIL = (("x", 1), ("y", 1), ("z", 2), ("z", 1))


def heads_of(part):
    return HEADS[part:] + HEADS[:part]


def mark_of(part):
    bits = [(axis, 0) for head in heads_of(part) for axis in head] + list(TAIL)
    code = 0
    for axis, bit in bits:
        own = code_of(lax.axis_index(axis), lax.axis_index("side"), SIZES[axis])
        code = code * 2 + ((own >> bit) & 1)
    return code


def turned(value, axis, d):
    return jnp.concatenate(
        [lax.slice_in_dim(value, k ^ d, (k ^ d) + 1, axis=axis) for k in range(4)], axis=axis
    )


def halves(value):
    n = value.shape[0] // 2
    return value[:n], value[n:].astype(BF16)


def sum_weights(sends, keeps):
    sums = []
    for part in range(PARTS):
        keep, send = keeps[part], sends[part]
        for step in range(len(HEADS)):
            value = keep.astype(F32) + trade(send, **heads_of(part)[step]).astype(F32)
            if step < len(HEADS) - 1:
                keep, send = halves(value)
        sums.append(value)
    value = jnp.stack(sums).reshape(PARTS, 4, 4, PIECE, 128)
    sent = value.astype(BF16)
    got = [trade(sent[:, d + 1], **flips) for d, flips in enumerate(PLANE_FOURS)]
    value = value[:, 0] + got[0].astype(F32) + got[1].astype(F32) + got[2].astype(F32)
    for bit, axis in ((4, 1), (2, 2)):
        mine = value.astype(BF16)
        got = trade(mine, z=bit).reshape(PARTS, 2, 2, PIECE, 128)
        mine = mine.astype(F32).reshape(PARTS, 2, 2, PIECE, 128)
        value = (mine + jnp.flip(got, axis).astype(F32)).reshape(PARTS, 4, PIECE, 128)
    return value.astype(BF16)


def spread_weights(value):
    value = jnp.concatenate([value] + [trade(value, **flips) for flips in PLANE_FOURS], axis=1)
    pairs = []
    for part in range(PARTS):
        mine = value[part]
        heads = heads_of(part)[::-1]
        for head in heads[:-1]:
            mine = jnp.concatenate([mine, trade(mine, **head)], axis=0)
        pairs += [mine, trade(mine, **heads[-1])]
    return pairs


FOURS = [({"z": 2 * d}, {"x": d}) for d in (1, 2, 3)]


def sum_all(keep, send, side):
    sent = swap(send)
    value = jnp.concatenate([sent + jnp.where(side == 0, keep, 0.0), keep])
    value = value.reshape(4, 4, TOK // 128, 1, 128)
    got = [turned(across(value, *flips), 1, d + 1) for d, flips in enumerate(FOURS)]
    value = (value + got[0]) + (got[1] + got[2])
    got = [turned(across(value, {"z": 1} if d == 1 else None, {"y": d}), 0, d) for d in (1, 2, 3)]
    value = ((value + got[0]) + (got[1] + got[2])).reshape(2 * LROWS, 1, 128)
    return value, swap(value[:LROWS])


def on_device(node_table, owner, local_row, w_in, w_mid, w_out):
    side = lax.axis_index("side").astype(jnp.int32)[None]
    place = jnp.stack([mark_of(part) for part in range(PARTS)]).astype(jnp.int32)
    table, weight_in, weight_mid, weight_out = node_table[0], w_in[0], w_mid[0], w_out[0]

    request, position = call(
        request_kernel,
        [((N_SHARD, 128), jnp.int32), ((1, TOK), jnp.int32)],
        [ANY, ANY],
        [pltpu.VMEM((1, TOK), jnp.int32)] * 2 + [pltpu.SemaphoreType.DMA((2,))],
        mib=63,
    )(owner.reshape(1, TOK), local_row)
    incoming = exchange(request.reshape(N_SHARD, 1, 128), ALL).reshape(N_SHARD, 128)
    (picked,) = call(
        pick_kernel,
        [((N_SHARD * LINES, WIDTH), BF16)],
        [VMEM, ANY],
        [
            pltpu.VMEM((ROWS_DEV, FEAT), BF16),
            pltpu.VMEM((WIDTH // 128, N_SHARD * LINES, 128), F32),
            pltpu.SemaphoreType.DMA((1,)),
        ],
    )(incoming, table)
    arrived = exchange(picked.reshape(N_SHARD, LINES, WIDTH), ALL).reshape(N_SHARD * LINES, WIDTH)
    weights = [pltpu.VMEM((FEAT, HID), BF16), pltpu.VMEM((HID, HID), BF16), pltpu.VMEM((HID, EMB), BF16)]
    x, u, r, e = call(
        forward_kernel,
        [
            ((TOK, FEAT), BF16), ((TOK, EMB), F32), ((TOK, EMB), F32), ((TOK, EMB), BF16),
        ],
        [VMEM, ANY, ANY, ANY, ANY],
        [pltpu.VMEM((N_SHARD * LINES, WIDTH), BF16)] + weights + [pltpu.SemaphoreType.DMA((4,))],
        mib=63,
    )(position, arrived, weight_in, weight_mid, weight_out)

    near = jnp.concatenate([e] + [across(e, *flips) for flips in FOURS])
    far = across(near, {"z": 1}, {"y": 1})
    rest = [across(near, None, {"y": d}) for d in (2, 3)]
    held, near_sent = lax.optimization_barrier((far, near))
    pieces = [near, far] + rest + [swap(near_sent), swap(held)]
    sums = call(
        sums_kernel, [((LROWS, 1, 128), F32)] * 2, [SMEM] + [VMEM] * 6, mib=32
    )(side, *pieces)
    sums = sum_all(*sums, side[0])

    keep, send, away = call(
        grad_kernel,
        [((UROWS, EMB), F32), ((UROWS, EMB), BF16), ((ICOLS, EMB), BF16)],
        [SMEM] + [VMEM] * 8,
        [pltpu.VMEM((CHUNK, ICOLS), F32), pltpu.VMEM((EMB, ICOLS), F32)],
        mib=32,
    )(side, *pieces, *sums)
    got = [across(away[(d - 2) * QUART:(d - 1) * QUART], None, {"y": d}) for d in (2, 3)]
    grad = jnp.where(side[0] == 0, keep, 0.0) + swap(send).astype(F32)
    got.append(across(grad[QUART:].astype(BF16), {"z": 1}, {"y": 1}))
    grad = grad[:QUART] + got[2].astype(F32) + got[0].astype(F32) + got[1].astype(F32)
    grad = grad.reshape(4, TOK, EMB)
    got = [across(grad[d + 1].astype(BF16), *flips) for d, flips in enumerate(FOURS)]

    wide = (TOK, HID)
    slopes = call(
        slopes_kernel,
        [(wide, BF16), (wide, BF16), (wide, F32), (wide, F32)],
        [VMEM, ANY, ANY],
        weights[:2] + [pltpu.SemaphoreType.DMA((2,))],
        mib=16,
    )(x, weight_in, weight_mid)
    slots = (SLOTS, PIECE, 128)
    sums = call(
        backward_kernel,
        [(slots, BF16)] * (2 * PARTS),
        [SMEM] + [VMEM] * 11 + [ANY] * 2,
        [pltpu.VMEM((WROWS, HID), F32)] + weights[1:] + [pltpu.SemaphoreType.DMA((2,))],
        mib=32,
    )(place, grad[0], *got, u, r, x, *slopes, weight_mid, weight_out)
    pairs = spread_weights(sum_weights(sums[:PARTS], sums[PARTS:]))
    grads = finish(tuple(range(PARTS)), 0, place, pairs[0::2], ())
    grads = finish(tuple(range(PARTS)), 1, place, pairs[1::2], grads)
    return tuple(g[None] for g in grads)


def solution(mesh):
    cube = Mesh(mesh.devices.reshape(2, NZ, NY, NX), ("side", "z", "y", "x"))
    rows = P("side", ALL, None)
    whole = P("side", None, None)
    return jax.shard_map(
        on_device,
        mesh=cube,
        in_specs=(rows, rows, P("side", ALL), whole, whole, whole),
        out_specs=(whole, whole, whole),
        check_vma=False,
    )
```

```python
import functools
import itertools
import math

import jax
import jax.numpy as jnp
from jax import lax
from jax.experimental import pallas as pl
from jax.experimental.pallas import tpu as pltpu
from jax.sharding import Mesh, PartitionSpec as P

NZ, NY, NX = 8, 4, 4
NYX = NY * NX
N_SHARD = NZ * NYX
CAP = 4
ROWS_DEV = 512
TOK = 256
FEAT, HID, EMB = 768, 1024, 128
SPLIT = 2
LINES = CAP * SPLIT
WIDTH = FEAT // SPLIT
TOKENS = N_SHARD * TOK
UROWS = NZ * TOK
ICOLS = NYX // 2 * TOK
QUART = 4 * TOK
EXP2_SCALE = 40.0 / math.log(2.0)
GRAD_SCALE = 40.0 * 0.5 / math.sqrt(TOKENS)
WROWS = FEAT + HID + EMB
PARTS = 3
PROWS = WROWS // PARTS
LANES = HID // 128
PIECE = PROWS * LANES // N_SHARD
BF16 = jnp.bfloat16
F32 = jnp.float32
VMEM = pl.BlockSpec(memory_space=pltpu.VMEM)
SMEM = pl.BlockSpec(memory_space=pltpu.SMEM)
ANY = pl.BlockSpec(memory_space=pl.ANY)


def call(kernel, outs, in_specs, scratch=(), mib=48, spaces=None):
    return pl.pallas_call(
        kernel,
        out_shape=[jax.ShapeDtypeStruct(s, d) for s, d in outs],
        in_specs=in_specs,
        out_specs=[pl.BlockSpec(memory_space=space) for space in spaces or [pltpu.VMEM] * len(outs)],
        scratch_shapes=list(scratch),
        compiler_params=pltpu.CompilerParams(vmem_limit_bytes=mib * 2**20),
    )


def dot(a, b, dims):
    return lax.dot_general(a, b, (dims, ((), ())), preferred_element_type=F32)


NN = ((1,), (0,))
NT = ((1,), (1,))
TN = ((0,), (0,))


def iota(shape, dim):
    return lax.broadcasted_iota(jnp.int32, shape, dim)


def begin(sources, targets, sems, first=0):
    copies = [
        pltpu.make_async_copy(source, target, sems.at[first + k])
        for k, (source, target) in enumerate(zip(sources, targets))
    ]
    for copy in copies:
        copy.start()
    return copies


def request_kernel(owner_any, wanted_any, request_ref, position_ref, owner_ref, wanted_ref, sems):
    for copy in begin([owner_any, wanted_any], [owner_ref, wanted_ref], sems):
        copy.wait()
    own_row = jnp.broadcast_to(owner_ref[...].astype(F32), (TOK, TOK))
    own_col = own_row.T
    earlier = iota((TOK, TOK), 0) < iota((TOK, TOK), 1)
    same = jnp.where((own_col == own_row) & earlier, 1.0, 0.0)
    rank = jnp.sum(same, axis=0, keepdims=True)
    owners = own_row[0:1, :]
    position_ref[...] = (owners * LINES + rank * SPLIT).astype(jnp.int32)
    wanted = wanted_ref[...].astype(F32) + 1.0
    owner_hit = iota((N_SHARD, TOK), 0).astype(F32) == owners
    lanes = iota((N_SHARD, 128), 1)
    request = jnp.zeros((N_SHARD, 128), F32)
    for k in range(CAP):
        hit = jnp.where(owner_hit & (rank == float(k)), wanted, 0.0)
        slot = jnp.sum(hit, axis=1, keepdims=True)
        request = jnp.where(lanes == k, slot, request)
    request_ref[...] = request.astype(jnp.int32) - 1


def pick_kernel(incoming_ref, table_any, picked_ref, table_ref, lines_ref, sems):
    (copy,) = begin([table_any], [table_ref], sems)
    slots = N_SHARD * CAP
    spread = jnp.where(iota((slots, N_SHARD), 0) // CAP == iota((slots, N_SHARD), 1), 1.0, 0.0)
    listed = lax.dot_general(
        spread,
        incoming_ref[...].astype(F32),
        (NN, ((), ())),
        precision=lax.Precision.HIGHEST,
        preferred_element_type=F32,
    )
    mine = iota((slots, 128), 0) % CAP == iota((slots, 128), 1)
    row = jnp.sum(jnp.where(mine, listed, 0.0), axis=1, keepdims=True)
    hit = jnp.where(row == iota((slots, ROWS_DEV), 1).astype(F32), 1.0, 0.0).astype(BF16)
    copy.wait()
    for h in range(SPLIT):
        for k in range(WIDTH // 128):
            lanes = slice(h * WIDTH + k * 128, h * WIDTH + (k + 1) * 128)
            lines_ref[k, pl.ds(h, slots, stride=SPLIT), :] = dot(hit, table_ref[:, lanes], NN)
    for k in range(WIDTH // 128):
        picked_ref[:, k * 128:(k + 1) * 128] = lines_ref[k].astype(BF16)


def finish(parts, half, place, halves, grads):
    n = len(parts)
    shapes = [(FEAT, HID), (HID, HID), (HID, EMB)]
    return pl.pallas_call(
        functools.partial(finish_kernel, parts, half),
        out_shape=[jax.ShapeDtypeStruct(shape, F32) for shape in shapes],
        in_specs=[SMEM] + [VMEM] * n + [ANY] * len(grads),
        out_specs=[ANY] * 3,
        scratch_shapes=[pltpu.VMEM((HROWS, HID), F32)] * n
        + [pltpu.VMEM((HID, EMB), F32), pltpu.SemaphoreType.DMA((2 * PARTS,))],
        input_output_aliases={1 + n + k: k for k in range(len(grads))},
        compiler_params=pltpu.CompilerParams(vmem_limit_bytes=16 * 2**20),
        cost_estimate=pl.CostEstimate(
            flops=0, transcendentals=0, bytes_accessed=n * SLOTS * PIECE * 128 * 6
        ),
    )(place, *halves, *grads)


def silu(v):
    return v * (1.0 / (1.0 + jnp.exp(-v)))


def slope(v):
    q = 1.0 / (1.0 + jnp.exp(-v))
    return q * (1.0 + v * (1.0 - q))


def forward_kernel(
    position_ref, arrived_any, w_in_any, w_mid_any, w_out_any,
    x_ref, u_ref, r_ref, e_ref, arrived_ref, w_in_ref, w_mid_ref, w_out_ref, sems,
):
    first = begin([arrived_any], [arrived_ref], sems, 3)
    loads = begin([w_in_any, w_mid_any, w_out_any], [w_in_ref, w_mid_ref, w_out_ref], sems)
    lines = iota((N_SHARD * LINES, TOK), 0)
    hits = [
        jnp.where(lines == position_ref[...] + h, 1.0, 0.0).astype(BF16) for h in range(SPLIT)
    ]
    first[0].wait()
    arrived = arrived_ref[...]
    x = jnp.concatenate([dot(hit, arrived, TN) for hit in hits], axis=1).astype(BF16)
    x_ref[...] = x
    loads[0].wait()
    z1 = dot(x, w_in_ref[...], NN)
    loads[1].wait()
    z2 = dot(silu(z1).astype(BF16), w_mid_ref[...], NN)
    loads[2].wait()
    z3 = dot(silu(z2).astype(BF16), w_out_ref[...], NN)
    r = lax.rsqrt(jnp.sum(z3 * z3, axis=1, keepdims=True) + 1e-6)
    u = z3 * r
    u_ref[...] = u
    r_ref[...] = jnp.broadcast_to(r, (TOK, EMB))
    e_ref[...] = u.astype(BF16)


CHUNK = TOK


def choose(side_ref, pieces):
    first = side_ref[0] == 0
    near, far, rest_near, rest_far, sent_near, sent_far = [piece[...] for piece in pieces]
    users = [jnp.where(first, near, sent_near), jnp.where(first, far, sent_far)]
    items = [jnp.where(first, sent_near, rest_near), jnp.where(first, sent_far, rest_far)]
    return users, jnp.concatenate(items, axis=0)


def rows_of(users, c):
    at = c * CHUNK % QUART
    return users[c * CHUNK // QUART][at:at + CHUNK, :]


LROWS = UROWS // 128


def sums_kernel(side_ref, *refs):
    keep_ref, send_ref = refs[6:]
    users, items = choose(side_ref, refs[:6])
    cols = jnp.zeros((8, ICOLS), F32)
    rows = []
    for c in range(NZ):
        expo = jnp.exp2(dot(rows_of(users, c), items, NT) * EXP2_SCALE)
        cols = cols + jnp.sum(expo.reshape(CHUNK // 8, 8, ICOLS), axis=0)
        folded = expo[:, 0:128]
        for k in range(1, ICOLS // 128):
            folded = folded + expo[:, k * 128:(k + 1) * 128]
        rows.append(jnp.sum(folded.T, axis=0, keepdims=True))
    rows = jnp.concatenate(rows, axis=1)
    cols = jnp.sum(cols, axis=0, keepdims=True)
    first = side_ref[0] == 0
    keep, send = jnp.where(first, rows, cols), jnp.where(first, cols, rows)
    for k in range(LROWS):
        keep_ref[k] = keep[:, k * 128:(k + 1) * 128]
        send_ref[k] = send[:, k * 128:(k + 1) * 128]


def grad_kernel(side_ref, *refs):
    total_ref, sent_ref, *outs, grad_ref, turned_ref = refs[6:]
    keep_refs, send_refs, away_refs = outs[0:2], outs[2:4], outs[4:6]
    users, items = choose(side_ref, refs[:6])
    first = side_ref[0] == 0
    col = [jnp.where(first, sent_ref[k], total_ref[LROWS + k]) for k in range(LROWS)]
    col_inv = 1.0 / jnp.concatenate(col, axis=1)
    for c in range(NZ):
        chunk = rows_of(users, c)
        scores = dot(chunk, items, NT)
        places = range(c * CHUNK // 128, (c + 1) * CHUNK // 128)
        totals = [jnp.where(first, total_ref[k], sent_ref[k]) for k in places]
        inv = jnp.broadcast_to(1.0 / jnp.concatenate(totals, axis=1), (128, CHUNK)).T[:, 0:1]
        grad_ref[...] = jnp.exp2(scores * EXP2_SCALE) * (inv + col_inv)
        if c == 0:
            own = jnp.where(first, 2.0, 0.0)
            eye = jnp.where(iota((TOK, TOK), 0) == iota((TOK, TOK), 1), own, 0.0)
            grad_ref[:, 0:TOK] = grad_ref[:, 0:TOK] - eye
        grad = grad_ref[...].astype(BF16)
        rows = slice(c * CHUNK % QUART, c * CHUNK % QUART + CHUNK)
        keep_refs[c * CHUNK // QUART][rows, :] = dot(grad, items, NN) * GRAD_SCALE
        term = dot(chunk, grad, TN)
        if c == 0:
            turned_ref[...] = term
        else:
            turned_ref[...] += term
    for c in range(NZ):
        half, rows = c * CHUNK // QUART, slice(c * CHUNK % QUART, c * CHUNK % QUART + CHUNK)
        of_items = (turned_ref[:, c * CHUNK:(c + 1) * CHUNK].T * GRAD_SCALE).astype(BF16)
        away_refs[half][rows, :] = of_items
        send_refs[half][rows, :] = jnp.where(first, of_items, keep_refs[half][rows, :].astype(BF16))


def piece_at(part, slot, code):
    piece = slot ^ code
    row = pl.multiple_of(part * PROWS + lax.shift_right_logical(piece, 3) * PIECE, 8)
    lane = pl.multiple_of(lax.bitwise_and(piece, LANES - 1) * 128, 128)
    return pl.ds(row, PIECE), pl.ds(lane, 128)


SLOTS = N_SHARD // 2


def slopes_kernel(
    x_ref, w_in_any, w_mid_any, h1_ref, h2_ref, s1_ref, s2_ref, w_in_ref, w_mid_ref, sems
):
    loads = begin([w_in_any, w_mid_any], [w_in_ref, w_mid_ref], sems)
    loads[0].wait()
    z1 = dot(x_ref[...], w_in_ref[...], NN)
    h1 = silu(z1).astype(BF16)
    h1_ref[...] = h1
    s1_ref[...] = slope(z1)
    loads[1].wait()
    z2 = dot(h1, w_mid_ref[...], NN)
    h2_ref[...] = silu(z2).astype(BF16)
    s2_ref[...] = slope(z2)


def backward_kernel(
    place_ref, keep_ref, sent0_ref, sent1_ref, sent2_ref, u_ref, r_ref,
    x_ref, h1_ref, h2_ref, s1_ref, s2_ref, w_mid_any, w_out_any, *rest,
):
    send_refs, keep_refs = rest[:PARTS], rest[PARTS:2 * PARTS]
    sums_ref, w_mid_ref, w_out_ref, sems = rest[2 * PARTS:]
    loads = begin([w_out_any, w_mid_any], [w_out_ref, w_mid_ref], sems)
    g = keep_ref[...] + sent0_ref[...].astype(F32)
    g = g + sent1_ref[...].astype(F32) + sent2_ref[...].astype(F32)
    u = u_ref[...]
    along = jnp.sum(g * u, axis=1, keepdims=True)
    dz3 = ((g - u * along) * r_ref[...]).astype(BF16)
    sums_ref[FEAT + HID:, :] = dot(dz3, h2_ref[...], TN)
    loads[0].wait()
    dz2 = (dot(dz3, w_out_ref[...], NT) * s2_ref[...]).astype(BF16)
    sums_ref[FEAT:FEAT + HID, :] = dot(h1_ref[...], dz2, TN)
    loads[1].wait()
    dz1 = (dot(dz2, w_mid_ref[...], NT) * s1_ref[...]).astype(BF16)
    sums_ref[0:FEAT, :] = dot(x_ref[...], dz1, TN)
    for part in range(PARTS):
        code = place_ref[part]
        for slot in range(SLOTS):
            keep_refs[part][slot] = sums_ref[piece_at(part, slot, code)].astype(BF16)
            send_refs[part][slot] = sums_ref[piece_at(part, SLOTS + slot, code)].astype(BF16)


HROWS = PROWS // 2
GRADS = ((0, FEAT), (FEAT, FEAT + HID), (FEAT + HID, WROWS))


def finish_kernel(parts, half, place_ref, *rest):
    n = len(parts)
    refs, rest = rest[:n], rest[n:] if half == 0 else rest[n + 3:]
    outs, rows_refs, turned_ref, sems = rest[:3], rest[3:3 + n], rest[3 + n], rest[4 + n]

    def copies_of(part, k, rows_ref, turn=True):
        base = part * PROWS + k * HROWS
        copies = []
        for out, (start, stop) in zip(outs, GRADS):
            low, high = max(start, base), min(stop, base + HROWS)
            if low >= high:
                continue
            source = rows_ref.at[low - base:high - base, :]
            target = out.at[low - start:high - start, :]
            if start == GRADS[2][0]:
                if turn:
                    turned_ref[...] = rows_ref[low - base:high - base, :].T
                source, target = turned_ref, out
            copies.append(pltpu.make_async_copy(source, target, sems.at[2 * part + len(copies)]))
        return copies

    for part, ref, rows_ref in zip(parts, refs, rows_refs):
        code = place_ref[part]
        for slot in range(SLOTS):
            piece = lax.bitwise_and(slot ^ code, SLOTS - 1)
            row = pl.multiple_of(lax.shift_right_logical(piece, 3) * PIECE, 8)
            lane = pl.multiple_of(lax.bitwise_and(piece, LANES - 1) * 128, 128)
            rows_ref[pl.ds(row, PIECE), pl.ds(lane, 128)] = ref[slot].astype(F32)
        for k in range(2):
            @pl.when((lax.shift_right_logical(code, 6) ^ half) == k)
            def _():
                for copy in copies_of(part, k, rows_ref):
                    copy.start()
    for part, rows_ref in zip(parts, rows_refs):
        for k in range(2):
            @pl.when((lax.shift_right_logical(place_ref[part], 6) ^ half) == k)
            def _():
                for copy in copies_of(part, k, rows_ref, False):
                    copy.wait()


ALL = ("z", "y", "x")
AXES = ("side",) + ALL
SIZES = {"side": 2, "z": NZ, "y": NY, "x": NX}
PLACES = list(itertools.product(*(range(SIZES[axis]) for axis in AXES)))
NUMBERS = {place: k for k, place in enumerate(PLACES)}


def exchange(value, axes):
    return lax.all_to_all(value, axes, split_axis=0, concat_axis=0, tiled=True)


def swap(value):
    return lax.ppermute(value, "side", [(0, 1), (1, 0)])


def gray(i):
    return i ^ (i >> 1)


def across(value, *flips):
    pairs = []
    for place, number in NUMBERS.items():
        if flips[place[0]] is None:
            continue
        other = []
        for axis, i in zip(AXES, place):
            at = {gray(k): k for k in range(SIZES[axis])}
            other.append(at[gray(i) ^ flips[place[0]].get(axis, 0)])
        pairs.append((number, NUMBERS[tuple(other)]))
    return lax.ppermute(value, AXES, pairs)


def both(value, **flips):
    return across(value, flips, flips)


def code_of(i, side, n):
    return gray((i + side) % n)


def trade(value, **flips):
    pairs = []
    for place, number in NUMBERS.items():
        other = [place[0]]
        for axis, i in zip(ALL, place[1:]):
            n = SIZES[axis]
            at = {code_of(k, place[0], n): k for k in range(n)}
            other.append(at[code_of(i, place[0], n) ^ flips.get(axis, 0)])
        pairs.append((number, NUMBERS[tuple(other)]))
    return lax.ppermute(value, AXES, pairs)


PLANE_FOURS = (dict(y=2), dict(x=2), dict(x=2, y=2))
HEADS = (dict(x=1), dict(y=1), dict(z=1))
TAIL = (("x", 1), ("y", 1), ("z", 2), ("z", 1))


def heads_of(part):
    return HEADS[part:] + HEADS[:part]


def mark_of(part):
    bits = [(axis, 0) for head in heads_of(part) for axis in head] + list(TAIL)
    code = 0
    for axis, bit in bits:
        own = code_of(lax.axis_index(axis), lax.axis_index("side"), SIZES[axis])
        code = code * 2 + ((own >> bit) & 1)
    return code


def turned(value, axis, d):
    return jnp.concatenate(
        [lax.slice_in_dim(value, k ^ d, (k ^ d) + 1, axis=axis) for k in range(4)], axis=axis
    )


def halves(value):
    n = value.shape[0] // 2
    return value[:n], value[n:].astype(BF16)


def sum_weights(sends, keeps):
    sums = []
    for part in range(PARTS):
        keep, send = keeps[part], sends[part]
        for step in range(len(HEADS)):
            value = keep.astype(F32) + trade(send, **heads_of(part)[step]).astype(F32)
            if step < len(HEADS) - 1:
                keep, send = halves(value)
        sums.append(value)
    value = jnp.stack(sums).reshape(PARTS, 4, 4, PIECE, 128)
    sent = value.astype(BF16)
    got = [trade(sent[:, d + 1], **flips) for d, flips in enumerate(PLANE_FOURS)]
    value = value[:, 0] + got[0].astype(F32) + got[1].astype(F32) + got[2].astype(F32)
    for bit, axis in ((4, 1), (2, 2)):
        mine = value.astype(BF16)
        got = trade(mine, z=bit).reshape(PARTS, 2, 2, PIECE, 128)
        mine = mine.astype(F32).reshape(PARTS, 2, 2, PIECE, 128)
        value = (mine + jnp.flip(got, axis).astype(F32)).reshape(PARTS, 4, PIECE, 128)
    return value.astype(BF16)


def spread_weights(value):
    value = jnp.concatenate([value] + [trade(value, **flips) for flips in PLANE_FOURS], axis=1)
    pairs = []
    for part in range(PARTS):
        mine = value[part]
        heads = heads_of(part)[::-1]
        for head in heads[:-1]:
            mine = jnp.concatenate([mine, trade(mine, **head)], axis=0)
        pairs += [mine, trade(mine, **heads[-1])]
    return pairs


FOURS = [({"z": 2 * d}, {"x": d}) for d in (1, 2, 3)]


def sum_all(keep, send, side):
    sent = swap(send)
    value = jnp.concatenate([sent + jnp.where(side == 0, keep, 0.0), keep])
    value = value.reshape(4, 4, TOK // 128, 1, 128)
    got = [turned(across(value, *flips), 1, d + 1) for d, flips in enumerate(FOURS)]
    value = (value + got[0]) + (got[1] + got[2])
    got = [turned(across(value, {"z": 1} if d == 1 else None, {"y": d}), 0, d) for d in (1, 2, 3)]
    value = ((value + got[0]) + (got[1] + got[2])).reshape(2 * LROWS, 1, 128)
    return value, swap(value[:LROWS])


def on_device(node_table, owner, local_row, w_in, w_mid, w_out):
    side = lax.axis_index("side").astype(jnp.int32)[None]
    place = jnp.stack([mark_of(part) for part in range(PARTS)]).astype(jnp.int32)
    table, weight_in, weight_mid, weight_out = node_table[0], w_in[0], w_mid[0], w_out[0]

    request, position = call(
        request_kernel,
        [((N_SHARD, 128), jnp.int32), ((1, TOK), jnp.int32)],
        [ANY, ANY],
        [pltpu.VMEM((1, TOK), jnp.int32)] * 2 + [pltpu.SemaphoreType.DMA((2,))],
        mib=63,
    )(owner.reshape(1, TOK), local_row)
    incoming = exchange(request.reshape(N_SHARD, 1, 128), ALL).reshape(N_SHARD, 128)
    (picked,) = call(
        pick_kernel,
        [((N_SHARD * LINES, WIDTH), BF16)],
        [VMEM, ANY],
        [
            pltpu.VMEM((ROWS_DEV, FEAT), BF16),
            pltpu.VMEM((WIDTH // 128, N_SHARD * LINES, 128), F32),
            pltpu.SemaphoreType.DMA((1,)),
        ],
    )(incoming, table)
    arrived = exchange(picked.reshape(N_SHARD, LINES, WIDTH), ALL).reshape(N_SHARD * LINES, WIDTH)
    weights = [pltpu.VMEM((FEAT, HID), BF16), pltpu.VMEM((HID, HID), BF16), pltpu.VMEM((HID, EMB), BF16)]
    x, u, r, e = call(
        forward_kernel,
        [
            ((TOK, FEAT), BF16), ((TOK, EMB), F32), ((TOK, EMB), F32), ((TOK, EMB), BF16),
        ],
        [VMEM, ANY, ANY, ANY, ANY],
        [pltpu.VMEM((N_SHARD * LINES, WIDTH), BF16)] + weights + [pltpu.SemaphoreType.DMA((4,))],
        mib=63,
    )(position, arrived, weight_in, weight_mid, weight_out)

    near = jnp.concatenate([e] + [across(e, *flips) for flips in FOURS])
    far = across(near, {"z": 1}, {"y": 1})
    rest = [across(near, None, {"y": d}) for d in (2, 3)]
    held, near_sent = lax.optimization_barrier((far, near))
    pieces = [near, far] + rest + [swap(near_sent), swap(held)]
    sums = call(
        sums_kernel, [((LROWS, 1, 128), F32)] * 2, [SMEM] + [VMEM] * 6, mib=32
    )(side, *pieces)
    sums = sum_all(*sums, side[0])

    *keep, send_near, send_far, away_two, away_three = call(
        grad_kernel,
        [((QUART, EMB), F32)] * 2 + [((QUART, EMB), BF16)] * 4,
        [SMEM] + [VMEM] * 8,
        [pltpu.VMEM((CHUNK, ICOLS), F32), pltpu.VMEM((EMB, ICOLS), F32)],
        mib=32,
    )(side, *pieces, *sums)
    got = [across(away_two, None, {"y": 2}), across(away_three, None, {"y": 3})]
    near, far = [
        jnp.where(side[0] == 0, mine, 0.0) + swap(send).astype(F32)
        for mine, send in zip(keep, (send_near, send_far))
    ]
    got.append(across(far.astype(BF16), {"z": 1}, {"y": 1}))
    grad = near + got[2].astype(F32) + got[0].astype(F32) + got[1].astype(F32)
    grad = grad.reshape(4, TOK, EMB)
    got = [across(grad[d + 1].astype(BF16), *flips) for d, flips in enumerate(FOURS)]

    wide = (TOK, HID)
    slopes = call(
        slopes_kernel,
        [(wide, BF16), (wide, BF16), (wide, F32), (wide, F32)],
        [VMEM, ANY, ANY],
        weights[:2] + [pltpu.SemaphoreType.DMA((2,))],
        mib=16,
    )(x, weight_in, weight_mid)
    slots = (SLOTS, PIECE, 128)
    sums = call(
        backward_kernel,
        [(slots, BF16)] * (2 * PARTS),
        [SMEM] + [VMEM] * 11 + [ANY] * 2,
        [pltpu.VMEM((WROWS, HID), F32)] + weights[1:] + [pltpu.SemaphoreType.DMA((2,))],
        mib=32,
    )(place, grad[0], *got, u, r, x, *slopes, weight_mid, weight_out)
    pairs = spread_weights(sum_weights(sums[:PARTS], sums[PARTS:]))
    grads = finish(tuple(range(PARTS)), 0, place, pairs[0::2], ())
    grads = finish((0,), 1, place, pairs[1:2], grads)
    grads = finish(tuple(range(1, PARTS)), 1, place, pairs[3::2], grads)
    return tuple(g[None] for g in grads)


def solution(mesh):
    cube = Mesh(mesh.devices.reshape(2, NZ, NY, NX), ("side", "z", "y", "x"))
    rows = P("side", ALL, None)
    whole = P("side", None, None)
    return jax.shard_map(
        on_device,
        mesh=cube,
        in_specs=(rows, rows, P("side", ALL), whole, whole, whole),
        out_specs=(whole, whole, whole),
        check_vma=False,
    )
```

```python
import functools
import itertools
import math

import jax
import jax.numpy as jnp
from jax import lax
from jax.experimental import pallas as pl
from jax.experimental.pallas import tpu as pltpu
from jax.sharding import Mesh, PartitionSpec as P

NZ, NY, NX = 8, 4, 4
NYX = NY * NX
N_SHARD = NZ * NYX
CAP = 4
ROWS_DEV = 512
TOK = 256
FEAT, HID, EMB = 768, 1024, 128
SPLIT = 2
LINES = CAP * SPLIT
WIDTH = FEAT // SPLIT
TOKENS = N_SHARD * TOK
UROWS = NZ * TOK
ICOLS = NYX // 2 * TOK
QUART = 4 * TOK
EXP2_SCALE = 40.0 / math.log(2.0)
GRAD_SCALE = 40.0 * 0.5 / math.sqrt(TOKENS)
WROWS = FEAT + HID + EMB
PARTS = 3
PROWS = WROWS // PARTS
LANES = HID // 128
PIECE = PROWS * LANES // N_SHARD
BF16 = jnp.bfloat16
F32 = jnp.float32
VMEM = pl.BlockSpec(memory_space=pltpu.VMEM)
SMEM = pl.BlockSpec(memory_space=pltpu.SMEM)
ANY = pl.BlockSpec(memory_space=pl.ANY)


def call(kernel, outs, in_specs, scratch=(), mib=48, spaces=None):
    return pl.pallas_call(
        kernel,
        out_shape=[jax.ShapeDtypeStruct(s, d) for s, d in outs],
        in_specs=in_specs,
        out_specs=[pl.BlockSpec(memory_space=space) for space in spaces or [pltpu.VMEM] * len(outs)],
        scratch_shapes=list(scratch),
        compiler_params=pltpu.CompilerParams(vmem_limit_bytes=mib * 2**20),
    )


def dot(a, b, dims):
    return lax.dot_general(a, b, (dims, ((), ())), preferred_element_type=F32)


NN = ((1,), (0,))
NT = ((1,), (1,))
TN = ((0,), (0,))


def iota(shape, dim):
    return lax.broadcasted_iota(jnp.int32, shape, dim)


def begin(sources, targets, sems, first=0):
    copies = [
        pltpu.make_async_copy(source, target, sems.at[first + k])
        for k, (source, target) in enumerate(zip(sources, targets))
    ]
    for copy in copies:
        copy.start()
    return copies


def request_kernel(owner_any, wanted_any, request_ref, position_ref, owner_ref, wanted_ref, sems):
    for copy in begin([owner_any, wanted_any], [owner_ref, wanted_ref], sems):
        copy.wait()
    own_row = jnp.broadcast_to(owner_ref[...].astype(F32), (TOK, TOK))
    own_col = own_row.T
    earlier = iota((TOK, TOK), 0) < iota((TOK, TOK), 1)
    same = jnp.where((own_col == own_row) & earlier, 1.0, 0.0)
    rank = jnp.sum(same, axis=0, keepdims=True)
    owners = own_row[0:1, :]
    position_ref[...] = (owners * LINES + rank * SPLIT).astype(jnp.int32)
    wanted = wanted_ref[...].astype(F32) + 1.0
    owner_hit = iota((N_SHARD, TOK), 0).astype(F32) == owners
    lanes = iota((N_SHARD, 128), 1)
    request = jnp.zeros((N_SHARD, 128), F32)
    for k in range(CAP):
        hit = jnp.where(owner_hit & (rank == float(k)), wanted, 0.0)
        slot = jnp.sum(hit, axis=1, keepdims=True)
        request = jnp.where(lanes == k, slot, request)
    request_ref[...] = request.astype(jnp.int32) - 1


def pick_kernel(incoming_ref, table_any, picked_ref, table_ref, lines_ref, sems):
    (copy,) = begin([table_any], [table_ref], sems)
    slots = N_SHARD * CAP
    spread = jnp.where(iota((slots, N_SHARD), 0) // CAP == iota((slots, N_SHARD), 1), 1.0, 0.0)
    listed = lax.dot_general(
        spread,
        incoming_ref[...].astype(F32),
        (NN, ((), ())),
        precision=lax.Precision.HIGHEST,
        preferred_element_type=F32,
    )
    mine = iota((slots, 128), 0) % CAP == iota((slots, 128), 1)
    row = jnp.sum(jnp.where(mine, listed, 0.0), axis=1, keepdims=True)
    hit = jnp.where(row == iota((slots, ROWS_DEV), 1).astype(F32), 1.0, 0.0).astype(BF16)
    copy.wait()
    for h in range(SPLIT):
        for k in range(WIDTH // 128):
            lanes = slice(h * WIDTH + k * 128, h * WIDTH + (k + 1) * 128)
            lines_ref[k, pl.ds(h, slots, stride=SPLIT), :] = dot(hit, table_ref[:, lanes], NN)
    for k in range(WIDTH // 128):
        picked_ref[:, k * 128:(k + 1) * 128] = lines_ref[k].astype(BF16)


def finish(parts, half, place, halves, grads):
    n = len(parts)
    shapes = [(FEAT, HID), (HID, HID), (HID, EMB)]
    return pl.pallas_call(
        functools.partial(finish_kernel, parts, half),
        out_shape=[jax.ShapeDtypeStruct(shape, F32) for shape in shapes],
        in_specs=[SMEM] + [VMEM] * n + [ANY] * len(grads),
        out_specs=[ANY] * 3,
        scratch_shapes=[pltpu.VMEM((HROWS, HID), F32)] * n
        + [pltpu.VMEM((HID, EMB), F32), pltpu.SemaphoreType.DMA((2 * PARTS,))],
        input_output_aliases={1 + n + k: k for k in range(len(grads))},
        compiler_params=pltpu.CompilerParams(vmem_limit_bytes=16 * 2**20),
        cost_estimate=pl.CostEstimate(
            flops=0, transcendentals=0, bytes_accessed=n * SLOTS * PIECE * 128 * 6
        ),
    )(place, *halves, *grads)


def silu(v):
    return v * (1.0 / (1.0 + jnp.exp(-v)))


def slope(v):
    q = 1.0 / (1.0 + jnp.exp(-v))
    return q * (1.0 + v * (1.0 - q))


def forward_kernel(
    position_ref, arrived_any, w_in_any, w_mid_any, w_out_any,
    x_ref, u_ref, r_ref, e_ref, arrived_ref, w_in_ref, w_mid_ref, w_out_ref, sems,
):
    first = begin([arrived_any], [arrived_ref], sems, 3)
    loads = begin([w_in_any, w_mid_any, w_out_any], [w_in_ref, w_mid_ref, w_out_ref], sems)
    lines = iota((N_SHARD * LINES, TOK), 0)
    hits = [
        jnp.where(lines == position_ref[...] + h, 1.0, 0.0).astype(BF16) for h in range(SPLIT)
    ]
    first[0].wait()
    arrived = arrived_ref[...]
    x = jnp.concatenate([dot(hit, arrived, TN) for hit in hits], axis=1).astype(BF16)
    x_ref[...] = x
    loads[0].wait()
    z1 = dot(x, w_in_ref[...], NN)
    loads[1].wait()
    z2 = dot(silu(z1).astype(BF16), w_mid_ref[...], NN)
    loads[2].wait()
    z3 = dot(silu(z2).astype(BF16), w_out_ref[...], NN)
    r = lax.rsqrt(jnp.sum(z3 * z3, axis=1, keepdims=True) + 1e-6)
    u = z3 * r
    u_ref[...] = u
    r_ref[...] = jnp.broadcast_to(r, (TOK, EMB))
    e_ref[...] = u.astype(BF16)


CHUNK = TOK


def choose(side_ref, pieces):
    first = side_ref[0] == 0
    near, far, rest_near, rest_far, sent_near, sent_far = [piece[...] for piece in pieces]
    users = [jnp.where(first, near, sent_near), jnp.where(first, far, sent_far)]
    items = [jnp.where(first, sent_near, rest_near), jnp.where(first, sent_far, rest_far)]
    return users, jnp.concatenate(items, axis=0)


def rows_of(users, c):
    at = c * CHUNK % QUART
    return users[c * CHUNK // QUART][at:at + CHUNK, :]


LROWS = UROWS // 128


def sums_kernel(side_ref, *refs):
    keep_ref, send_ref = refs[6:]
    users, items = choose(side_ref, refs[:6])
    cols = jnp.zeros((8, ICOLS), F32)
    rows = []
    for c in range(NZ):
        expo = jnp.exp2(dot(rows_of(users, c), items, NT) * EXP2_SCALE)
        cols = cols + jnp.sum(expo.reshape(CHUNK // 8, 8, ICOLS), axis=0)
        folded = expo[:, 0:128]
        for k in range(1, ICOLS // 128):
            folded = folded + expo[:, k * 128:(k + 1) * 128]
        rows.append(jnp.sum(folded.T, axis=0, keepdims=True))
    rows = jnp.concatenate(rows, axis=1)
    cols = jnp.sum(cols, axis=0, keepdims=True)
    first = side_ref[0] == 0
    keep, send = jnp.where(first, rows, cols), jnp.where(first, cols, rows)
    for k in range(LROWS):
        keep_ref[k] = keep[:, k * 128:(k + 1) * 128]
        send_ref[k] = send[:, k * 128:(k + 1) * 128]


def grad_kernel(side_ref, *refs):
    total_ref, sent_ref, *outs, grad_ref, turned_ref = refs[6:]
    keep_refs, send_refs, away_refs = outs[0:2], outs[2:4], outs[4:6]
    users, items = choose(side_ref, refs[:6])
    first = side_ref[0] == 0
    col = [jnp.where(first, sent_ref[k], total_ref[LROWS + k]) for k in range(LROWS)]
    col_inv = 1.0 / jnp.concatenate(col, axis=1)
    for c in range(NZ):
        chunk = rows_of(users, c)
        scores = dot(chunk, items, NT)
        places = range(c * CHUNK // 128, (c + 1) * CHUNK // 128)
        totals = [jnp.where(first, total_ref[k], sent_ref[k]) for k in places]
        inv = jnp.broadcast_to(1.0 / jnp.concatenate(totals, axis=1), (128, CHUNK)).T[:, 0:1]
        grad_ref[...] = jnp.exp2(scores * EXP2_SCALE) * (inv + col_inv)
        if c == 0:
            own = jnp.where(first, 2.0, 0.0)
            eye = jnp.where(iota((TOK, TOK), 0) == iota((TOK, TOK), 1), own, 0.0)
            grad_ref[:, 0:TOK] = grad_ref[:, 0:TOK] - eye
        grad = grad_ref[...].astype(BF16)
        rows = slice(c * CHUNK % QUART, c * CHUNK % QUART + CHUNK)
        keep_refs[c * CHUNK // QUART][rows, :] = dot(grad, items, NN) * GRAD_SCALE
        term = dot(chunk, grad, TN)
        if c == 0:
            turned_ref[...] = term
        else:
            turned_ref[...] += term
    for c in range(NZ):
        half, rows = c * CHUNK // QUART, slice(c * CHUNK % QUART, c * CHUNK % QUART + CHUNK)
        of_items = (turned_ref[:, c * CHUNK:(c + 1) * CHUNK].T * GRAD_SCALE).astype(BF16)
        away_refs[half][rows, :] = of_items
        send_refs[half][rows, :] = jnp.where(first, of_items, keep_refs[half][rows, :].astype(BF16))


def piece_at(part, slot, code):
    piece = slot ^ code
    row = pl.multiple_of(part * PROWS + lax.shift_right_logical(piece, 3) * PIECE, 8)
    lane = pl.multiple_of(lax.bitwise_and(piece, LANES - 1) * 128, 128)
    return pl.ds(row, PIECE), pl.ds(lane, 128)


SLOTS = N_SHARD // 2


def slopes_kernel(
    x_ref, w_in_any, w_mid_any, h1_ref, h2_ref, s1_ref, s2_ref, w_in_ref, w_mid_ref, sems
):
    loads = begin([w_in_any, w_mid_any], [w_in_ref, w_mid_ref], sems)
    loads[0].wait()
    z1 = dot(x_ref[...], w_in_ref[...], NN)
    h1 = silu(z1).astype(BF16)
    h1_ref[...] = h1
    s1_ref[...] = slope(z1)
    loads[1].wait()
    z2 = dot(h1, w_mid_ref[...], NN)
    h2_ref[...] = silu(z2).astype(BF16)
    s2_ref[...] = slope(z2)


def backward_kernel(
    place_ref, keep_ref, sent0_ref, sent1_ref, sent2_ref, u_ref, r_ref,
    x_ref, h1_ref, h2_ref, s1_ref, s2_ref, w_mid_any, w_out_any, *rest,
):
    send_refs, keep_refs = rest[:PARTS], rest[PARTS:2 * PARTS]
    sums_ref, w_mid_ref, w_out_ref, sems = rest[2 * PARTS:]
    loads = begin([w_out_any, w_mid_any], [w_out_ref, w_mid_ref], sems)
    g = keep_ref[...] + sent0_ref[...].astype(F32)
    g = g + sent1_ref[...].astype(F32) + sent2_ref[...].astype(F32)
    u = u_ref[...]
    along = jnp.sum(g * u, axis=1, keepdims=True)
    dz3 = ((g - u * along) * r_ref[...]).astype(BF16)
    sums_ref[FEAT + HID:, :] = dot(dz3, h2_ref[...], TN)
    loads[0].wait()
    dz2 = (dot(dz3, w_out_ref[...], NT) * s2_ref[...]).astype(BF16)
    sums_ref[FEAT:FEAT + HID, :] = dot(h1_ref[...], dz2, TN)
    loads[1].wait()
    dz1 = (dot(dz2, w_mid_ref[...], NT) * s1_ref[...]).astype(BF16)
    sums_ref[0:FEAT, :] = dot(x_ref[...], dz1, TN)
    for part in range(PARTS):
        code = place_ref[part]
        for slot in range(SLOTS):
            keep_refs[part][slot] = sums_ref[piece_at(part, slot, code)].astype(BF16)
            send_refs[part][slot] = sums_ref[piece_at(part, SLOTS + slot, code)].astype(BF16)


HROWS = PROWS // 2
GRADS = ((0, FEAT), (FEAT, FEAT + HID), (FEAT + HID, WROWS))


def finish_kernel(parts, half, place_ref, *rest):
    n = len(parts)
    refs, rest = rest[:n], rest[n:] if half == 0 else rest[n + 3:]
    outs, rows_refs, turned_ref, sems = rest[:3], rest[3:3 + n], rest[3 + n], rest[4 + n]

    def copies_of(part, k, rows_ref, turn=True):
        base = part * PROWS + k * HROWS
        copies = []
        for out, (start, stop) in zip(outs, GRADS):
            low, high = max(start, base), min(stop, base + HROWS)
            if low >= high:
                continue
            source = rows_ref.at[low - base:high - base, :]
            target = out.at[low - start:high - start, :]
            if start == GRADS[2][0]:
                if turn:
                    turned_ref[...] = rows_ref[low - base:high - base, :].T
                source, target = turned_ref, out
            copies.append(pltpu.make_async_copy(source, target, sems.at[2 * part + len(copies)]))
        return copies

    for part, ref, rows_ref in zip(parts, refs, rows_refs):
        code = place_ref[part]
        for slot in range(SLOTS):
            piece = lax.bitwise_and(slot ^ code, SLOTS - 1)
            row = pl.multiple_of(lax.shift_right_logical(piece, 3) * PIECE, 8)
            lane = pl.multiple_of(lax.bitwise_and(piece, LANES - 1) * 128, 128)
            rows_ref[pl.ds(row, PIECE), pl.ds(lane, 128)] = ref[slot].astype(F32)
        for k in range(2):
            @pl.when((lax.shift_right_logical(code, 6) ^ half) == k)
            def _():
                for copy in copies_of(part, k, rows_ref):
                    copy.start()
    for part, rows_ref in zip(parts, rows_refs):
        for k in range(2):
            @pl.when((lax.shift_right_logical(place_ref[part], 6) ^ half) == k)
            def _():
                for copy in copies_of(part, k, rows_ref, False):
                    copy.wait()


ALL = ("z", "y", "x")
AXES = ("side",) + ALL
SIZES = {"side": 2, "z": NZ, "y": NY, "x": NX}
PLACES = list(itertools.product(*(range(SIZES[axis]) for axis in AXES)))
NUMBERS = {place: k for k, place in enumerate(PLACES)}


def exchange(value, axes):
    return lax.all_to_all(value, axes, split_axis=0, concat_axis=0, tiled=True)


def swap(value):
    return lax.ppermute(value, "side", [(0, 1), (1, 0)])


def gray(i):
    return i ^ (i >> 1)


def across(value, *flips):
    pairs = []
    for place, number in NUMBERS.items():
        if flips[place[0]] is None:
            continue
        other = []
        for axis, i in zip(AXES, place):
            at = {gray(k): k for k in range(SIZES[axis])}
            other.append(at[gray(i) ^ flips[place[0]].get(axis, 0)])
        pairs.append((number, NUMBERS[tuple(other)]))
    return lax.ppermute(value, AXES, pairs)


def both(value, **flips):
    return across(value, flips, flips)


def code_of(i, side, n):
    return gray((i + side) % n)


def trade(value, **flips):
    pairs = []
    for place, number in NUMBERS.items():
        other = [place[0]]
        for axis, i in zip(ALL, place[1:]):
            n = SIZES[axis]
            at = {code_of(k, place[0], n): k for k in range(n)}
            other.append(at[code_of(i, place[0], n) ^ flips.get(axis, 0)])
        pairs.append((number, NUMBERS[tuple(other)]))
    return lax.ppermute(value, AXES, pairs)


PLANE_FOURS = (dict(y=2), dict(x=2), dict(x=2, y=2))
HEADS = (dict(x=1), dict(y=1), dict(z=1))
TAIL = (("x", 1), ("y", 1), ("z", 2), ("z", 1))


def heads_of(part):
    return HEADS[part:] + HEADS[:part]


def mark_of(part):
    bits = [(axis, 0) for head in heads_of(part) for axis in head] + list(TAIL)
    code = 0
    for axis, bit in bits:
        own = code_of(lax.axis_index(axis), lax.axis_index("side"), SIZES[axis])
        code = code * 2 + ((own >> bit) & 1)
    return code


def turned(value, axis, d):
    return jnp.concatenate(
        [lax.slice_in_dim(value, k ^ d, (k ^ d) + 1, axis=axis) for k in range(4)], axis=axis
    )


def halves(value):
    n = value.shape[0] // 2
    return value[:n], value[n:].astype(BF16)


def sum_weights(sends, keeps):
    sums = []
    for part in range(PARTS):
        keep, send = keeps[part], sends[part]
        for step in range(len(HEADS)):
            value = keep.astype(F32) + trade(send, **heads_of(part)[step]).astype(F32)
            if step < len(HEADS) - 1:
                keep, send = halves(value)
        sums.append(value)
    value = jnp.stack(sums).reshape(PARTS, 4, 4, PIECE, 128)
    sent = value.astype(BF16)
    got = [trade(sent[:, d + 1], **flips) for d, flips in enumerate(PLANE_FOURS)]
    value = value[:, 0] + got[0].astype(F32) + got[1].astype(F32) + got[2].astype(F32)
    for bit, axis in ((4, 1), (2, 2)):
        mine = value.astype(BF16)
        got = trade(mine, z=bit).reshape(PARTS, 2, 2, PIECE, 128)
        mine = mine.astype(F32).reshape(PARTS, 2, 2, PIECE, 128)
        value = (mine + jnp.flip(got, axis).astype(F32)).reshape(PARTS, 4, PIECE, 128)
    return value.astype(BF16)


def spread_weights(value):
    value = jnp.concatenate([value] + [trade(value, **flips) for flips in PLANE_FOURS], axis=1)
    pairs = []
    for part in range(PARTS):
        mine = value[part]
        heads = heads_of(part)[::-1]
        for head in heads[:-1]:
            mine = jnp.concatenate([mine, trade(mine, **head)], axis=0)
        pairs += [mine, trade(mine, **heads[-1])]
    return pairs


FOURS = [({"z": 2 * d}, {"x": d}) for d in (1, 2, 3)]


def sum_all(keep, send, side):
    sent = swap(send)
    value = jnp.concatenate([sent + jnp.where(side == 0, keep, 0.0), keep])
    value = value.reshape(4, 4, TOK // 128, 1, 128)
    got = [turned(across(value, *flips), 1, d + 1) for d, flips in enumerate(FOURS)]
    value = (value + got[0]) + (got[1] + got[2])
    got = [turned(across(value, {"z": 1} if d == 1 else None, {"y": d}), 0, d) for d in (1, 2, 3)]
    value = ((value + got[0]) + (got[1] + got[2])).reshape(2 * LROWS, 1, 128)
    return value, swap(value[:LROWS])


def on_device(node_table, owner, local_row, w_in, w_mid, w_out):
    side = lax.axis_index("side").astype(jnp.int32)[None]
    place = jnp.stack([mark_of(part) for part in range(PARTS)]).astype(jnp.int32)
    table, weight_in, weight_mid, weight_out = node_table[0], w_in[0], w_mid[0], w_out[0]

    request, position = call(
        request_kernel,
        [((N_SHARD, 128), jnp.int32), ((1, TOK), jnp.int32)],
        [ANY, ANY],
        [pltpu.VMEM((1, TOK), jnp.int32)] * 2 + [pltpu.SemaphoreType.DMA((2,))],
        mib=63,
    )(owner.reshape(1, TOK), local_row)
    incoming = exchange(request.reshape(N_SHARD, 1, 128), ALL).reshape(N_SHARD, 128)
    (picked,) = call(
        pick_kernel,
        [((N_SHARD * LINES, WIDTH), BF16)],
        [VMEM, ANY],
        [
            pltpu.VMEM((ROWS_DEV, FEAT), BF16),
            pltpu.VMEM((WIDTH // 128, N_SHARD * LINES, 128), F32),
            pltpu.SemaphoreType.DMA((1,)),
        ],
    )(incoming, table)
    arrived = exchange(picked.reshape(N_SHARD, LINES, WIDTH), ALL).reshape(N_SHARD * LINES, WIDTH)
    weights = [pltpu.VMEM((FEAT, HID), BF16), pltpu.VMEM((HID, HID), BF16), pltpu.VMEM((HID, EMB), BF16)]
    x, u, r, e = call(
        forward_kernel,
        [
            ((TOK, FEAT), BF16), ((TOK, EMB), F32), ((TOK, EMB), F32), ((TOK, EMB), BF16),
        ],
        [VMEM, ANY, ANY, ANY, ANY],
        [pltpu.VMEM((N_SHARD * LINES, WIDTH), BF16)] + weights + [pltpu.SemaphoreType.DMA((4,))],
        mib=63,
    )(position, arrived, weight_in, weight_mid, weight_out)

    near = jnp.concatenate([e] + [across(e, *flips) for flips in FOURS])
    far = across(near, {"z": 1}, {"y": 1})
    rest = [across(near, None, {"y": d}) for d in (2, 3)]
    held, near_sent = lax.optimization_barrier((far, near))
    pieces = [near, far] + rest + [swap(near_sent), swap(held)]
    sums = call(
        sums_kernel, [((LROWS, 1, 128), F32)] * 2, [SMEM] + [VMEM] * 6, mib=32
    )(side, *pieces)
    sums = sum_all(*sums, side[0])

    *keep, send_near, send_far, away_two, away_three = call(
        grad_kernel,
        [((QUART, EMB), F32)] * 2 + [((QUART, EMB), BF16)] * 4,
        [SMEM] + [VMEM] * 8,
        [pltpu.VMEM((CHUNK, ICOLS), F32), pltpu.VMEM((EMB, ICOLS), F32)],
        mib=32,
    )(side, *pieces, *sums)
    got = [across(away_two, None, {"y": 2}), across(away_three, None, {"y": 3})]
    near, far = [
        jnp.where(side[0] == 0, mine, 0.0) + swap(send).astype(F32)
        for mine, send in zip(keep, (send_near, send_far))
    ]
    got.append(across(far.astype(BF16), {"z": 1}, {"y": 1}))
    grad = near + got[2].astype(F32) + got[0].astype(F32) + got[1].astype(F32)
    grad = grad.reshape(4, TOK, EMB)
    got = [across(grad[d + 1].astype(BF16), *flips) for d, flips in enumerate(FOURS)]

    wide = (TOK, HID)
    slopes = call(
        slopes_kernel,
        [(wide, BF16), (wide, BF16), (wide, F32), (wide, F32)],
        [VMEM, ANY, ANY],
        weights[:2] + [pltpu.SemaphoreType.DMA((2,))],
        mib=16,
    )(x, weight_in, weight_mid)
    slots = (SLOTS, PIECE, 128)
    sums = call(
        backward_kernel,
        [(slots, BF16)] * (2 * PARTS),
        [SMEM] + [VMEM] * 11 + [ANY] * 2,
        [pltpu.VMEM((WROWS, HID), F32)] + weights[1:] + [pltpu.SemaphoreType.DMA((2,))],
        mib=32,
    )(place, grad[0], *got, u, r, x, *slopes, weight_mid, weight_out)
    pairs = spread_weights(sum_weights(sums[:PARTS], sums[PARTS:]))
    grads = finish(tuple(range(PARTS)), 0, place, pairs[0::2], ())
    grads = finish((1,), 1, place, pairs[3:4], grads)
    grads = finish((0, 2), 1, place, pairs[1::4], grads)
    return tuple(g[None] for g in grads)


def solution(mesh):
    cube = Mesh(mesh.devices.reshape(2, NZ, NY, NX), ("side", "z", "y", "x"))
    rows = P("side", ALL, None)
    whole = P("side", None, None)
    return jax.shard_map(
        on_device,
        mesh=cube,
        in_specs=(rows, rows, P("side", ALL), whole, whole, whole),
        out_specs=(whole, whole, whole),
        check_vma=False,
    )
```
